512 devices in a mesh: lat: 8 (over x, z_lo), lon: 64 (over y, z_hi, core).
Axes of the slice: x: 4, y: 8, z: 8 (z_hi: 4, z_lo: 2; z = z_hi * 2 + z_lo), core: 2. Of those that a mesh axis runs over, the one named last changes fastest.
Arguments:
- fields: bfloat16 [4, 96, 768, 192], P(None, 'lat', 'lon'), may hold values from -6 to 6
- region_one: int32 [4, 96, 768], P(None, 'lat', 'lon'), may hold values from 0 to 3
- region_two: int32 [4, 48, 384], P(None, 'lat', 'lon'), may hold values from 0 to 3
- valid_rows: int32 [96], replicated, may hold values 0 or 1
- gain_one: float32 [192], replicated, may hold values from 0.1 to 1.9
- project_one: bfloat16 [192, 576], replicated, may hold values from -0.4375 to 0.4375
- output_one: bfloat16 [192, 192], replicated, may hold values from -0.4375 to 0.4375
- table_one: bfloat16 [16, 2, 6, 3312], P('lat'), may hold values from -4 to 305
- gain_two: float32 [192], replicated, may hold values from 0.1 to 1.9
- up_weight: bfloat16 [192, 768], replicated, may hold values from -0.4375 to 0.4375
- down_weight: bfloat16 [768, 192], replicated, may hold values from -0.21875 to 0.21875
- gain_three: float32 [768], replicated, may hold values from 0.1 to 1.9
- merge_weight: bfloat16 [768, 384], replicated, may hold values from -0.21875 to 0.21875
- gain_four: float32 [384], replicated, may hold values from 0.1 to 1.9
- project_two: bfloat16 [384, 1152], replicated, may hold values from -0.3125 to 0.3125
- output_two: bfloat16 [384, 384], replicated, may hold values from -0.3125 to 0.3125
- table_two: bfloat16 [8, 2, 12, 3312], P('lat'), may hold values from -4 to 305
Outputs:
- refined: bfloat16 [4, 48, 384, 384], P(None, 'lat', 'lon')
The draws below stay inside these ranges and needn't reach their ends.
All inputs are finite; a program needn't handle non-finite values.
Results may differ from the reference program's by a relative error of at most 0.019.
Values may be sent and summed in bfloat16 or wider, within the bound.
A program may use at most 64 MiB of HBM per device.

```python
from functools import partial
import jax
import jax.numpy as jnp
import numpy as np
from jax import lax

NZ = 4
D1 = 192
H1 = 6
MLP = 768
D2 = 384
H2 = 12
WZ = 2
WLAT = 6
WLON = 12
NLAT = 96
NLON = 768


def draw_table_one(key, part):
    key = jax.random.fold_in(key, 17)
    table_shape = (NLAT // WLAT, NZ // WZ, H1, WZ * WZ * WLAT * WLAT * (2 * WLON - 1))
    key_one = jax.random.fold_in(key, 0)
    values = jnp.clip(jax.random.normal(key_one, table_shape, jnp.float32), -4.0, 4.0)
    return values.astype(jnp.bfloat16)


def draw_table_two(key, part):
    key = jax.random.fold_in(key, 23)
    table_shape = (NLAT // (2 * WLAT), NZ // WZ, H2, WZ * WZ * WLAT * WLAT * (2 * WLON - 1))
    key_one = jax.random.fold_in(key, 0)
    values = jnp.clip(jax.random.normal(key_one, table_shape, jnp.float32), -4.0, 4.0)
    return values.astype(jnp.bfloat16)


def set_ends(values, stream_key, low, high):
    longest = values.shape.index(max(values.shape))
    spots = []
    for shift in (0, 1):
        where = [jax.random.randint(jax.random.fold_in(stream_key, axis), (), 0, length) for axis, length in enumerate(values.shape)]
        where[longest] = (where[longest] + shift) % values.shape[longest]
        spots.append(tuple(where))
    return values.at[spots[0]].set(low).at[spots[1]].set(high)


def block_levels(rng, extent, cuts, smallest, high):
    def one(dim, shards_of):
        steps = jax.random.uniform(jax.random.fold_in(jax.random.fold_in(rng, 6), dim), (shards_of,), jnp.float32, smallest / len(cuts), high / len(cuts))
        return jnp.repeat(jnp.exp(steps), extent[dim] // shards_of).reshape((-1,) + (1,) * (len(extent) - dim - 1))

    gain = one(*cuts[0])
    for cut in cuts[1:]:
        gain = gain * one(*cut)
    return gain


def noise(own_key, dims, width, bound, shards=(), kind=jnp.bfloat16):
    values = width * jax.random.normal(own_key, dims, jnp.float32)
    if shards:
        values = values * block_levels(own_key, dims, shards, -0.22, 0.18)
    return jnp.clip(values, -bound, bound).astype(kind)


def setup_inputs(seed: int = 0) -> dict:
    key_list = jax.random.split(jax.random.key(seed), 18)
    return {
        "fields": noise(key_list[0], (NZ, NLAT, NLON, D1), 1.0, 6.0, ((1, 8), (2, 64))),
        "region_one": set_ends(jax.random.randint(key_list[1], (NZ, NLAT, NLON), 0, 4), jax.random.fold_in(key_list[1], 1), 0, 3).astype(jnp.int32),
        "region_two": set_ends(jax.random.randint(key_list[2], (NZ, NLAT // 2, NLON // 2), 0, 4), jax.random.fold_in(key_list[2], 1), 0, 3).astype(jnp.int32),
        "valid_rows": set_ends((jax.random.randint(key_list[3], (NLAT,), 0, 8) < 7).astype(jnp.int32), jax.random.fold_in(key_list[3], 1), 0, 1),
        "gain_one": jnp.clip(1.0 + 0.18 * jax.random.normal(key_list[4], (D1,), jnp.float32), 0.1, 1.9),
        "project_one": noise(key_list[5], (D1, 3 * D1), D1 ** -0.5, 0.4375),
        "output_one": noise(key_list[6], (D1, D1), D1 ** -0.5, 0.4375),
        "table_one": draw_table_one(jax.random.fold_in(key_list[17], 71), 0),
        "gain_two": jnp.clip(1.0 + 0.18 * jax.random.normal(key_list[8], (D1,), jnp.float32), 0.1, 1.9),
        "up_weight": noise(key_list[9], (D1, MLP), D1 ** -0.5, 0.4375),
        "down_weight": noise(key_list[10], (MLP, D1), MLP ** -0.5, 0.21875),
        "gain_three": jnp.clip(1.0 + 0.18 * jax.random.normal(key_list[11], (4 * D1,), jnp.float32), 0.1, 1.9),
        "merge_weight": noise(key_list[12], (4 * D1, D2), (4 * D1) ** -0.5, 0.21875),
        "gain_four": jnp.clip(1.0 + 0.18 * jax.random.normal(key_list[13], (D2,), jnp.float32), 0.1, 1.9),
        "project_two": noise(key_list[14], (D2, 3 * D2), D2 ** -0.5, 0.3125),
        "output_two": noise(key_list[15], (D2, D2), D2 ** -0.5, 0.3125),
        "table_two": draw_table_two(jax.random.fold_in(key_list[17], 71), 0),
    }


def position_index():
    window_size = WZ * WLAT * WLON
    places = np.arange(window_size)
    level_pos = places // (WLAT * WLON)
    band_pos = places // WLON % WLAT
    sector = places % WLON
    pair_index = ((level_pos[:, None] * WZ + level_pos[None, :]) * (WLAT * WLAT) + band_pos[:, None] * WLAT + band_pos[None, :]) * (2 * WLON - 1) + sector[:, None] - sector[None, :] + WLON - 1
    return pair_index.astype(np.int32)

def to_windows(field):
    levels, lat_rows, lon_cols, feature_width = field.shape
    split = field.reshape(levels // WZ, WZ, lat_rows // WLAT, WLAT, lon_cols // WLON, WLON, feature_width)
    return split.transpose(2, 0, 4, 1, 3, 5, 6).reshape(lat_rows // WLAT, levels // WZ, lon_cols // WLON, WZ * WLAT * WLON, feature_width)

def from_windows(windows, levels, lat_rows, lon_cols):
    feature_width = windows.shape[-1]
    split = windows.reshape(lat_rows // WLAT, levels // WZ, lon_cols // WLON, WZ, WLAT, WLON, feature_width)
    return split.transpose(1, 3, 0, 4, 2, 5, 6).reshape(levels, lat_rows, lon_cols, feature_width)

def normalize(field, gain_vec):
    values = field.astype(jnp.float32)
    center = lax.optimization_barrier(jnp.mean(values, -1, keepdims=True))
    spread = lax.optimization_barrier(jnp.mean((values - center) ** 2, -1, keepdims=True))
    return (values - center) * lax.rsqrt(spread + 1e-05) * gain_vec.astype(jnp.float32)

def window_attention(normed, project, output, bias_table, region, key_valid, head_count):
    levels, lat_rows, lon_cols, feature_width = normed.shape
    head_size = feature_width // head_count
    window_size = WZ * WLAT * WLON
    index_table = position_index()
    eye_mask = jnp.eye(window_size, dtype=bool)
    windows = to_windows(normed)
    region_win = to_windows(region[..., None])[..., 0]
    valid_full = jnp.broadcast_to(key_valid[None, :, None, None], (levels, lat_rows, lon_cols, 1))
    valid_win = to_windows(valid_full)[..., 0]

    def one_band(operands):
        tokens_win, table_win, region_band, valid_band = operands
        level_count = tokens_win.shape[0]
        sector_count = tokens_win.shape[1]
        flat = tokens_win.reshape(-1, feature_width)
        mixed = jnp.dot(flat, project, preferred_element_type=jnp.float32).astype(jnp.bfloat16)
        mixed = mixed.reshape(level_count, sector_count, window_size, 3, head_count, head_size)
        queries = mixed[:, :, :, 0].astype(jnp.float32)
        key_vecs = mixed[:, :, :, 1].astype(jnp.float32)
        value_vecs = mixed[:, :, :, 2].astype(jnp.float32)
        scores = jnp.einsum('zwqhd,zwkhd->zwhqk', queries, key_vecs) * head_size ** (-0.5)
        bias = jnp.take(table_win, index_table, axis=2).astype(jnp.float32)
        scores = scores + bias[:, None]
        allowed = (region_band[..., :, None] == region_band[..., None, :]) & ((valid_band[..., None, :] == 1) | eye_mask)
        allowed = allowed[:, :, None]
        top_score = lax.optimization_barrier(jnp.max(jnp.where(allowed, scores, -jnp.inf), -1, keepdims=True))
        weights = jnp.where(allowed, jnp.exp(scores - top_score), 0.0)
        probs = (weights / lax.optimization_barrier(jnp.sum(weights, -1, keepdims=True))).astype(jnp.bfloat16)
        heads_out = jnp.einsum('zwhqk,zwkhd->zwqhd', probs.astype(jnp.float32), value_vecs).astype(jnp.bfloat16)
        heads_out = heads_out.reshape(-1, feature_width)
        projected = jnp.dot(heads_out, output, preferred_element_type=jnp.float32).astype(jnp.bfloat16)
        return projected.reshape(level_count, sector_count, window_size, feature_width)
    result = lax.map(one_band, (windows, bias_table, region_win, valid_win))
    return from_windows(result, levels, lat_rows, lon_cols)

def feed_forward(state, gain_vec, up_weight, down_weight):
    feature_width = state.shape[-1]
    normed = normalize(state, gain_vec).astype(jnp.bfloat16).reshape(-1, feature_width)
    inner = jax.nn.gelu(jnp.dot(normed, up_weight, preferred_element_type=jnp.float32), approximate=False).astype(jnp.bfloat16)
    grown = jnp.dot(inner, down_weight, preferred_element_type=jnp.float32).reshape(state.shape)
    return (state.astype(jnp.float32) + grown).astype(jnp.bfloat16)

def merge_patches(field, gain_vec, merge_weight):
    levels, lat_rows, lon_cols, feature_width = field.shape
    patches = field.reshape(levels, lat_rows // 2, 2, lon_cols // 2, 2, feature_width)
    patches = patches.transpose(0, 1, 3, 2, 4, 5).reshape(levels, lat_rows // 2, lon_cols // 2, 4 * feature_width)
    normed = normalize(patches, gain_vec).astype(jnp.bfloat16).reshape(-1, 4 * feature_width)
    coarse = jnp.dot(normed, merge_weight, preferred_element_type=jnp.float32).astype(jnp.bfloat16)
    return coarse.reshape(levels, lat_rows // 2, lon_cols // 2, merge_weight.shape[1])

def reference(fields, region_one, region_two, valid_rows, gain_one, project_one, output_one, table_one, gain_two, up_weight, down_weight, gain_three, merge_weight, gain_four, project_two, output_two, table_two):
    forward_shift = (-(WZ // 2), -(WLAT // 2), -(WLON // 2))
    backward_shift = (WZ // 2, WLAT // 2, WLON // 2)
    rolled = jnp.roll(fields, forward_shift, (0, 1, 2))
    normed_one = normalize(rolled, gain_one).astype(jnp.bfloat16)
    keep_one = jnp.roll(valid_rows, -(WLAT // 2))
    attended_one = window_attention(normed_one, project_one, output_one, table_one, region_one, keep_one, H1)
    attended_one = jnp.roll(attended_one, backward_shift, (0, 1, 2))
    state = (fields.astype(jnp.float32) + attended_one.astype(jnp.float32)).astype(jnp.bfloat16)
    block_out = lax.map(partial(feed_forward, gain_vec=gain_two, up_weight=up_weight, down_weight=down_weight), state)
    coarse = merge_patches(block_out, gain_three, merge_weight)
    coarse_valid = jnp.maximum(valid_rows[0::2], valid_rows[1::2])
    keep_two = jnp.roll(coarse_valid, -(WLAT // 2))
    rolled_two = jnp.roll(coarse, forward_shift, (0, 1, 2))
    normed_four = normalize(rolled_two, gain_four).astype(jnp.bfloat16)
    attended_two = window_attention(normed_four, project_two, output_two, table_two, region_two, keep_two, H2)
    attended_two = jnp.roll(attended_two, backward_shift, (0, 1, 2))
    return (coarse.astype(jnp.float32) + attended_two.astype(jnp.float32)).astype(jnp.bfloat16)
```

```python
import functools

import jax
import jax.numpy as jnp
import ml_dtypes
import numpy as np
from jax import lax
from jax.experimental import pallas as pl
from jax.experimental.pallas import tpu as pltpu
from jax.sharding import PartitionSpec as P

D1, H1, MLP = 192, 6, 768
D2, H2 = 384, 12
HEAD = 32
LIVE = 36
HELD = 48
KEYS = 4 * LIVE
COLUMN = 6 * LIVE
PAIRS = 3312
SPAN = 6 * 23
TABLE = 3456
FAR = 2.0**100
MESH = pl.DeviceIdType.MESH
LEVELS = ((1, 2), (3, 0))
FEATURE = 64


def atom_rows():
    return [((z * 3 + a) * 6 + o, z, a, o) for z in range(2) for a in range(3) for o in range(6)]


@functools.lru_cache(None)
def constants():
    split = np.zeros((2, 2, 40, 3, 12, 8), np.float32)
    for level in range(2):
        for og in range(2):
            for r, z, a, o in atom_rows():
                split[level, og, r, a, og * 6 + o, LEVELS[level][z]] = 1

    def spread(heads):
        rows = np.zeros((6, heads, 6, HELD), np.float32)
        for r, z, a, o in atom_rows():
            rows[o, :, z * 3 + a, r] = 1
        return rows.reshape(-1, HELD)

    def head_mask(heads, lanes):
        mask = np.zeros((6, heads, 6, lanes), np.float32)
        for h in range(heads):
            mask[:, h, :, h * HEAD : (h + 1) * HEAD] = 1
        mask[..., heads * HEAD :] = 1
        return mask.reshape(-1, lanes)

    def choose(heads, padded):
        sel = np.zeros((2, 2, heads, 6, 2, 6, padded), np.float32)
        for level in range(2):
            for s in range(2):
                for h in range(heads):
                    for za in range(6):
                        sel[level, s, h, za, s, za, 2 * h + level] = 1
        return sel.reshape(4 * heads * 6, 2 * 6 * padded)

    shift = np.zeros((2, 3, 512, KEYS), np.float32)
    for half in range(2):
        for pair in range(3):
            oq = 6 * half + 2 * pair
            for ah in range(2):
                for oh in range(2):
                    for r, z, a, o in atom_rows():
                        lane = z * 256 + (3 * ah + a) * 23 + oq - (6 * oh + o) + 11
                        shift[half, pair, lane, (oh * 2 + ah) * LIVE + r] = 1

    repeat = np.zeros((128, 128), np.float32)
    level_lanes = np.zeros((12, 8, 128), np.float32)
    gather = np.zeros((16, 12, 8), np.float32)
    for z in range(4):
        for n in range(32):
            repeat[n, z * 32 + n] = 1
        level_lanes[:, z, z * 32 : z * 32 + 32] = 1
        for a in range(12):
            gather[a, a, z] = 1
    rows_one = np.zeros((COLUMN, 32), np.float32)
    rows_two = np.zeros((COLUMN, 32), np.float32)
    table = np.zeros((11, COLUMN, 128), np.float32)
    table[8:10, :, FEATURE : FEATURE + 4] = 1
    table[8:10, :, FEATURE + 5 : FEATURE + 25] = 1
    for ag in range(6):
        for r, z, a, o in atom_rows():
            k = ag * LIVE + r
            window, ah = ag // 2, ag % 2
            rows_one[k, (0 if window == 0 else 16) + (6, 0, 6)[window] + 3 * ah + a] = 1
            if ag < 4:
                rows_two[k, 16 * window + 3 * ah + a] = 1
            table[10, k, :] = 3 * ag + a
            for level in range(2):
                table[4 + level, k, (2 * level + z) * 32 + 16 + o] = 1
                for oh in range(2):
                    table[2 * level + oh, k, (2 * level + z) * 32 + 6 * oh + o] = 1
            for oh in range(2):
                for at in (5 + z, 7 + 3 * ah + a, 13 + 6 * oh + o):
                    table[6 + oh, k, FEATURE + at] = 1
                    table[8 + oh, k, FEATURE + at] = 0

    merge = np.zeros((4, 2, LIVE, 2, 4, LIVE), np.float32)
    for da in range(2):
        for do in range(2):
            for half in range(2):
                for r, z, a, o in atom_rows():
                    row, col = 2 * (3 * half + a) + da, 2 * o + do
                    at = (z * 3 + row % 3) * 6 + col % 6
                    merge[da * 2 + do, half, r, col // 6, row // 3, at] = 1
    final = np.zeros((6, 6, 8, 2, 2, LIVE), np.float32)
    for level in range(2):
        for half in range(2):
            for r, z, a, o in atom_rows():
                final[3 * half + a, o, LEVELS[level][z], level, half, r] = 1
    b = lambda x: x.astype(ml_dtypes.bfloat16)
    flip = lambda x: np.concatenate([x.T[:LIVE], np.zeros((4, x.shape[0]), np.float32)])
    return dict(
        split=b(split.reshape(160, 288)),
        repeat=b(repeat),
        level_lanes=level_lanes.reshape(96, 128),
        gather=b(gather.reshape(16, 96)),
        choose_one=b(choose(H1, 16)),
        choose_two=b(choose(H2, 24)),
        shift=b(shift),
        rows_one=b(rows_one),
        rows_two=b(rows_two),
        table=table,
        spread_one=b(spread(H1)),
        heads_one=b(head_mask(H1, 256)),
        back_one=b(flip(spread(H1))),
        merge=b(merge.reshape(288, 288)),
        spread_two=b(spread(H2)),
        heads_two=b(head_mask(H2, 512)),
        back_two=b(flip(spread(H2))),
        final=b(final.reshape(288, 144)),
    )


CONST_NAMES = tuple(constants())
ARG_NAMES = (
    "fields",
    "region_one",
    "region_two",
    "valid",
    "gain_one",
    "project_one",
    "output_one",
    "table_one",
    "gain_two",
    "up",
    "down",
    "gain_three",
    "merge_weight",
    "gain_four",
    "project_two",
    "output_two",
    "table_two",
)
FETCHED = (
    "fields",
    "split",
    "region_one",
    "region_two",
    "repeat",
    "level_lanes",
    "gather",
    "table_one",
    "choose_one",
    "shift",
    "project_one",
    "rows_one",
    "table",
    "table_two",
    "choose_two",
    "spread_one",
    "heads_one",
    "back_one",
    "output_one",
    "up",
    "down",
    "merge",
    "merge_weight",
    "project_two",
    "rows_two",
    "spread_two",
    "heads_two",
    "back_two",
    "output_two",
    "final",
)


def dot(a, b):
    return jnp.dot(a, b, preferred_element_type=jnp.float32)


def dot_t(a, b):
    return lax.dot_general(a, b, (((1,), (1,)), ((), ())), preferred_element_type=jnp.float32)


def bf(x):
    return x.astype(jnp.bfloat16)


def normalize(x, gain):
    x = x.astype(jnp.float32)
    x = x - jnp.mean(x, -1, keepdims=True)
    var = jnp.mean(x * x, -1, keepdims=True)
    return bf(x * lax.rsqrt(var + 1e-5) * gain)


def attend(q, spread, head_mask, key, bias, value, back):
    q = bf(dot(spread, bf(q))) * head_mask
    scores = dot_t(q, key) + bias
    weights = jnp.exp(scores - jnp.max(scores, -1, keepdims=True))
    probs = bf(weights * (1.0 / jnp.sum(weights, -1, keepdims=True)))
    mixed = bf(dot(probs, value)) * head_mask[:, 0 : value.shape[1]]
    return dot(back, mixed)[0:LIVE]


def kernel(lat_size, lon_size, names, scratch_names, *refs):
    g = dict(zip((*names, "out", *scratch_names), refs, strict=True))
    send, recv, load = g["send"], g["recv"], g["load"]
    lat, lon = lax.axis_index("lat"), lax.axis_index("lon")
    odd = lax.rem(lon, 2)
    half_own = 1 - odd

    def at(dlat, dlon):
        return (lax.rem(lat + dlat + lat_size, lat_size), lax.rem(lon + dlon + lon_size, lon_size))

    around = [(a, o) for a in (-1, 0, 1) for o in (-1, 0, 1) if (a, o) != (0, 0)]
    barrier = pltpu.get_barrier_semaphore()
    for a, o in around + [(0, -2), (-1, -2)]:
        pl.semaphore_signal(barrier, inc=1, device_id=at(a, o), device_id_type=MESH)

    loads = {}
    for n, name in enumerate(FETCHED):
        loads[name] = pltpu.make_async_copy(g[name], g["vmem_" + name], load.at[n])
        loads[name].start()
    ready = set()

    def v(name):
        if name not in loads:
            return g[name]
        if name not in ready:
            loads[name].wait()
            ready.add(name)
        return g["vmem_" + name]

    copies = []

    def start(src, dst, target):
        n = len(copies)
        copy = pltpu.make_async_remote_copy(
            src_ref=src, dst_ref=dst, send_sem=send.at[n], recv_sem=recv.at[n], device_id=target, device_id_type=MESH
        )
        copies.append(copy)
        copy.start()
        return copy

    ext, rows_in = g["ext"], g["rows_in"]
    rows_in[...] = jnp.zeros_like(rows_in)
    for a in range(12):
        rows_in[a, :, 0:4, :] = v("fields")[a].astype(jnp.float32)
    for ag in range(4):
        moved = dot(v("split")[...], bf(rows_in[3 * ag : 3 * ag + 3].reshape(288, D1)))
        for level in range(2):
            for og in range(2):
                lo = (level * 2 + og) * 40
                ext[level, 1 + og, (1 + ag) * LIVE : (2 + ag) * LIVE, :] = moved[lo : lo + LIVE]

    def pack_level(level):
        for og in range(2):
            x = ext[level, 1 + og, LIVE : 5 * LIVE, :]
            tail = jnp.concatenate([x[0:72, 128:192], x[72:144, 128:192]], 1)
            tail = jnp.concatenate([tail, jnp.zeros((8, 128), jnp.float32)], 0)
            g["send_lon"][level, og] = bf(jnp.concatenate([x[:, 0:128], tail], 0))
        for end in range(2):
            lo = (1 + 3 * end) * LIVE
            x, y = ext[level, 1, lo : lo + 40, :], ext[level, 2, lo : lo + 40, :]
            tail = jnp.concatenate([x[:, 128:192], y[:, 128:192]], 1)
            g["send_lat"][level, end] = bf(
                jnp.concatenate([x[:, 0:128], y[:, 0:128], tail, jnp.zeros((8, 128), jnp.float32)], 0)
            )
            zero = jnp.zeros((40, 64), jnp.float32)
            for og, part in enumerate((x, y)):
                g["send_corner"][level, 2 * end + og] = bf(
                    jnp.concatenate([part[:, 0:128], jnp.concatenate([part[:, 128:192], zero], 1)], 0)
                )

    def send_level(level):
        lon_s, lat_s, cor_s = g["send_lon"], g["send_lat"], g["send_corner"]
        lon_r, lat_r, cor_r = g["recv_lon"], g["recv_lat"], g["recv_corner"]
        return [
            start(lon_s.at[level, 0], lon_r.at[level, 1], at(0, -1)),
            start(lon_s.at[level, 1], lon_r.at[level, 0], at(0, 1)),
            start(lat_s.at[level, 0], lat_r.at[level, 1], at(-1, 0)),
            start(lat_s.at[level, 1], lat_r.at[level, 0], at(1, 0)),
            start(cor_s.at[level, 0], cor_r.at[level, 3], at(-1, -1)),
            start(cor_s.at[level, 1], cor_r.at[level, 2], at(-1, 1)),
            start(cor_s.at[level, 2], cor_r.at[level, 1], at(1, -1)),
            start(cor_s.at[level, 3], cor_r.at[level, 0], at(1, 1)),
        ]

    def unpack_level(level):
        for side in range(2):
            x = g["recv_lon"][level, side].astype(jnp.float32)
            c = 3 * side
            ext[level, c, LIVE : 5 * LIVE, 0:128] = x[0:144]
            ext[level, c, LIVE : 3 * LIVE, 128:192] = x[144:216, 0:64]
            ext[level, c, 3 * LIVE : 5 * LIVE, 128:192] = x[144:216, 64:128]
            for end in range(2):
                y = g["recv_corner"][level, 2 * end + side].astype(jnp.float32)
                lo = 5 * LIVE * end
                ext[level, c, lo : lo + LIVE, 0:128] = y[0:LIVE]
                ext[level, c, lo : lo + LIVE, 128:192] = y[40 : 40 + LIVE, 0:64]
        for end in range(2):
            x = g["recv_lat"][level, end].astype(jnp.float32)
            lo = 5 * LIVE * end
            for og in range(2):
                ext[level, 1 + og, lo : lo + LIVE, 0:128] = x[og * 40 : og * 40 + LIVE]
                ext[level, 1 + og, lo : lo + LIVE, 128:192] = x[80 : 80 + LIVE, og * 64 : og * 64 + 64]

    pack_level(0)
    pl.semaphore_wait(barrier, 10)
    first = [send_level(0)]

    ids, region = g["ids"], g["region"]
    region[...] = jnp.zeros_like(region)
    region[:, 0:4, 0:12] = v("region_one")[...].astype(jnp.float32)
    region[0:6, 0:4, 16:22] = v("region_two")[...].astype(jnp.float32)
    packed = dot(bf(region[...].reshape(96, 128)), v("repeat")[...]) * v("level_lanes")[...]
    ids[0] = bf(dot(v("gather")[...], bf(packed)))
    id_copies = [
        start(ids.at[0], ids.at[1], at(1, 0)),
        start(ids.at[0], ids.at[2], at(0, 1)),
        start(ids.at[0], ids.at[3], at(1, 1)),
        start(ids.at[0], ids.at[4], at(0, 2)),
        start(ids.at[0], ids.at[5], at(1, 2)),
    ]
    table_copy_one = start(v("table_one").at[1], g["table_in_one"], at(1, 0))
    pack_level(1)
    first.append(send_level(1))
    table_copy_two = start(v("table_two").at[0], g["table_in_two"], at(1, 0))

    lane_one = lax.broadcasted_iota(jnp.int32, (D1, 256), 1)
    weight = v("project_one")[...].astype(jnp.float32)
    weight_kv, weight_q = g["weight_kv"], g["weight_q"]
    shifted = pltpu.roll(weight[:, 128:512], 384 - 64, 1)[:, 0:256]
    weight_kv[:, 0:256] = bf(jnp.where(lane_one < D1, shifted, 0.0))
    weight_kv[:, 256:448] = bf(weight[:, 384:576])
    weight_q[...] = bf(jnp.where(lane_one < D1, weight[:, 0:256], 0.0))

    def window_rows(flat, window, first_row):
        parts = []
        for shift in range(2):
            for zq in range(2):
                for aq in range(first_row, first_row + 3):
                    pieces = []
                    for zk in range(2):
                        offset = ((zq * 2 + zk) * 6 + aq) * SPAN + shift
                        base = offset // 128 * 128
                        piece = flat[window, :, base : base + 384]
                        if offset != base:
                            piece = pltpu.roll(piece, 384 - (offset - base), 1)
                        pieces.append(piece[:, 0:256])
                    parts.append(jnp.concatenate(pieces, 1))
        return bf(jnp.concatenate(parts, 0))

    flat_one, flat_two = g["flat_one"], g["flat_two"]
    left_one, left_two, bias_one, bias_two = g["left_one"], g["left_two"], g["bias_one"], g["bias_two"]
    flat_one[...] = jnp.zeros_like(flat_one)
    flat_two[...] = jnp.zeros_like(flat_two)

    def fill_one(ag):
        window, first_row = ((0, 3), (1, 0), (1, 3), (2, 0))[ag]
        part = dot(v("choose_one")[...], window_rows(flat_one, window, first_row))
        for level in range(2):
            left_one[level * 288 + ag * 72 : level * 288 + ag * 72 + 72] = part[level * 72 : level * 72 + 72]

    def fill_two(ag):
        part = dot(v("choose_two")[...], window_rows(flat_two, ag, 3 - 3 * ag))
        for level in range(2):
            lo = (level * 2 + ag) * 144
            left_two[lo : lo + 144] = part[level * 144 : level * 144 + 144]

    for h in range(H1):
        for window in (1, 2):
            flat_one[window, 2 * h : 2 * h + 2, 0:PAIRS] = v("table_one")[window - 1, h].astype(jnp.float32)
    for ag in (1, 2, 3):
        fill_one(ag)
    for h in range(H2):
        flat_two[1, 2 * h : 2 * h + 2, 0:PAIRS] = v("table_two")[0, h].astype(jnp.float32)
    fill_two(1)
    table_copy_one.wait_recv()
    for h in range(H1):
        flat_one[0, 2 * h : 2 * h + 2, 0:PAIRS] = g["table_in_one"][h].astype(jnp.float32)
    fill_one(0)
    left = bf(left_one[...])
    for og in range(2):
        for pair in range(3):
            part = dot(left, v("shift")[1 - og, pair])
            for block in range(8):
                bias_one[block, og, pair * 72 : pair * 72 + 72] = part[block * 72 : block * 72 + 72]

    for copy in id_copies:
        copy.wait_recv()
    table = v("table")
    valid = g["valid"][...]
    rows_global = valid.shape[1]
    lane_valid = lax.broadcasted_iota(jnp.int32, (COLUMN, rows_global), 1)
    lane_number = lax.broadcasted_iota(jnp.int32, (COLUMN, 128), 1).astype(jnp.float32)
    row_here = table[10, :, 0:rows_global].astype(jnp.int32)

    def wrap(row, extent):
        return jnp.where(row >= extent, row - extent, row)

    row = wrap(lax.rem(12 * lat + rows_global - 3, rows_global) + row_here, rows_global)
    alive = jnp.sum(jnp.where((lane_valid == row) & (valid == 1), 1.0, 0.0), -1, keepdims=True)
    row = wrap(lax.rem(6 * lat + rows_global // 2 - 3, rows_global // 2) + row_here, rows_global // 2)
    alive_two = jnp.max(jnp.where((lane_valid >> 1 == row) & (valid == 1), 1.0, 0.0), -1, keepdims=True)
    for side in range(2):
        mine = jnp.concatenate([ids[3 - 2 * side], ids[2 - 2 * side]], 0)
        picked = dot(v("rows_one")[...], mine)
        for level in range(2):
            for oh in range(2):
                c = 2 * side + oh
                number = jnp.sum(picked * table[2 * level + oh], -1, keepdims=True)
                same = jnp.where(number + FEATURE == lane_number, 1.0, 0.0)
                g["key_mask"][level, c] = same + (1.0 - alive) * table[6 + oh]
                if c in (1, 2):
                    g["query_mask"][level, c - 1] = (table[8 + oh] - same) * (-FAR)
    for oh in range(2):
        slot = 2 * half_own + 2 - 2 * oh
        mine = jnp.concatenate([ids[slot + 1], ids[slot]], 0)
        picked = dot(v("rows_two")[...], mine)
        for level in range(2):
            number = jnp.sum(picked * table[4 + level], -1, keepdims=True)
            same = jnp.where(number + FEATURE == lane_number, 1.0, 0.0)
            g["key_mask_two"][level, oh] = same + (1.0 - alive_two) * table[6 + oh]
            g["query_mask_two"][level, oh] = (table[8 + oh] - same) * (-FAR)

    kv, queries, heads = g["kv"], g["queries"], g["heads"]

    def section_one(level):
        for c in range(4):
            normed = normalize(ext[level, c], g["gain_one"][...])
            part = dot(normed, weight_kv[...])
            kv[c, :, 0:128] = part[:, 0:128]
            kv[c, :, 128:256] = part[:, 128:256] + g["key_mask"][level, c]
            kv[c, :, 256:448] = part[:, 256:448]
            if c in (1, 2):
                q = dot(normed, weight_q[...]) * HEAD ** (-0.5)
                queries[c - 1, :, 0:128] = q[:, 0:128]
                queries[c - 1, :, 128:256] = q[:, 128:256] + g["query_mask"][level, c - 1]
        for side in range(2):
            for window in range(3):
                lo = window * 72
                both = [kv[2 * side + oh, lo : lo + 72, :] for oh in range(2)]
                both = bf(jnp.concatenate(both, 0))
                key, value = both[:, 0:256], both[:, 256:448]
                for ah in ((1,), (0, 1), (0,))[window]:
                    ag = 2 * window + ah - 1
                    part = attend(
                        queries[side, (ag + 1) * LIVE : (ag + 1) * LIVE + HELD, :],
                        v("spread_one")[...],
                        v("heads_one")[...],
                        key,
                        bias_one[level * 4 + ag, side],
                        value,
                        v("back_one")[...],
                    )
                    base = side * 144 + ag * LIVE
                    heads[base : base + LIVE] = part
        attended = bf(dot(bf(heads[...]), v("output_one")[...]))
        own = jnp.concatenate([ext[level, 1 + og, LIVE : 5 * LIVE, :] for og in range(2)], 0)
        state = bf(own + attended.astype(jnp.float32))
        normed = normalize(state, g["gain_two"][...])
        inner = dot(normed, v("up")[...])
        inner = bf(0.5 * inner * (1.0 + lax.erf(inner * 0.5**0.5)))
        block = bf(state.astype(jnp.float32) + dot_t(inner, v("down")[...]))
        parts = [dot(v("merge")[n * 72 : n * 72 + 72], block) for n in range(4)]
        center = sum(jnp.sum(p, -1, keepdims=True) for p in parts) / (4 * D1)
        parts = [p - center for p in parts]
        scale = lax.rsqrt(sum(jnp.sum(p * p, -1, keepdims=True) for p in parts) / (4 * D1) + 1e-5)
        gain = g["gain_three"][...].reshape(1, 4 * D1)
        coarse = sum(
            dot(bf(parts[n] * scale * gain[:, n * D1 : n * D1 + D1]), v("merge_weight")[n * D1 : n * D1 + D1])
            for n in range(4)
        )
        coarse = bf(coarse).astype(jnp.float32)
        g["ext_two"][level, half_own, LIVE : 3 * LIVE, :] = coarse
        g["coarse"][level] = coarse
        zero = jnp.zeros((8, D2), jnp.float32)
        g["send_all"][level] = bf(jnp.concatenate([coarse, zero], 0))
        g["send_end"][level, 0] = bf(jnp.concatenate([coarse[0:40], zero], 0))
        g["send_end"][level, 1] = bf(jnp.concatenate([coarse[32:72], zero], 0))
        to = 2 * odd - 1
        ends, into = g["send_end"], g["recv_end"]
        return [
            start(g["send_all"].at[level], g["recv_all"].at[level], at(0, to)),
            start(ends.at[level, 0], into.at[level, 0, 1], at(-1, 0)),
            start(ends.at[level, 1], into.at[level, 0, 0], at(1, 0)),
            start(ends.at[level, 0], into.at[level, 1, 1], at(-1, to)),
            start(ends.at[level, 1], into.at[level, 1, 0], at(1, to)),
        ]

    def own_queries(level):
        q = dot(normalize(g["coarse"][level], g["gain_four"][...].reshape(1, D2)), v("project_two")[:, 0:D2]) * HEAD ** (-0.5)
        g["queries_two"][level, 0:72, 0:D2] = q
        g["queries_two"][level, 0:72, D2:512] = g["query_mask_two"][level, half_own, LIVE : 3 * LIVE, :]
        g["queries_two"][level, 72:96, :] = jnp.zeros((24, 512), jnp.float32)

    kv_two, heads_two, ext_two = g["kv_two"], g["heads_two_out"], g["ext_two"]

    def section_two(level):
        ext_two[level, odd, LIVE : 3 * LIVE, :] = g["recv_all"][level].astype(jnp.float32)[0:72]
        for who, oh in ((0, half_own), (1, odd)):
            ext_two[level, oh, 0:LIVE, :] = g["recv_end"][level, who, 0].astype(jnp.float32)[4:40]
            ext_two[level, oh, 3 * LIVE : 4 * LIVE, :] = g["recv_end"][level, who, 1].astype(jnp.float32)[0:LIVE]
        for oh in range(2):
            normed = normalize(ext_two[level, oh], g["gain_four"][...].reshape(1, D2))
            part = dot(normed, v("project_two")[:, D2:])
            kv_two[oh, :, 0:D2] = part[:, 0:D2]
            kv_two[oh, :, D2:512] = g["key_mask_two"][level, oh, 0:144]
            kv_two[oh, :, 512:896] = part[:, D2:]
        for ag in range(2):
            both = bf(jnp.concatenate([kv_two[oh, ag * 72 : ag * 72 + 72, :] for oh in range(2)], 0))
            part = attend(
                g["queries_two"][level, ag * LIVE : ag * LIVE + HELD, :],
                v("spread_two")[...],
                v("heads_two")[...],
                both[:, 0:512],
                bias_two[level * 2 + ag],
                both[:, 512:896],
                v("back_two")[...],
            )
            heads_two[level, ag * LIVE : ag * LIVE + LIVE] = part
        attended = bf(dot(bf(heads_two[level]), v("output_two")[...]))
        return g["coarse"][level] + attended.astype(jnp.float32)

    def wait_all(group):
        for copy in group:
            copy.wait_recv()

    wait_all(first[0])
    unpack_level(0)
    second = [section_one(0)]
    own_queries(0)
    wait_all(first[1])
    unpack_level(1)
    second.append(section_one(1))
    own_queries(1)

    table_copy_two.wait_recv()
    for h in range(H2):
        flat_two[0, 2 * h : 2 * h + 2, 0:PAIRS] = g["table_in_two"][h].astype(jnp.float32)
    fill_two(0)
    left = bf(left_two[...])
    for pair in range(3):
        part = dot(left, v("shift")[half_own, pair])
        for block in range(4):
            bias_two[block, pair * 144 : pair * 144 + 144] = part[block * 144 : block * 144 + 144]

    wait_all(second[0])
    refined = [section_two(0)]
    wait_all(second[1])
    refined.append(section_two(1))
    placed = dot(v("final")[...], bf(jnp.concatenate(refined, 0))).reshape(36, 8, D2)
    for i in range(6):
        g["out"][i] = bf(placed[6 * i : 6 * i + 6, 0:4])
    for copy in copies:
        copy.wait_send()


def shards(lat_size, lon_size, *args):
    operands = dict(zip(ARG_NAMES, args, strict=True))
    for name in ("valid", "gain_one", "gain_two"):
        operands[name] = operands[name][None]
    operands["fields"] = operands["fields"].transpose(1, 2, 0, 3)
    for name in ("region_one", "region_two"):
        operands[name] = operands[name].transpose(1, 0, 2)
    for name in ("table_one", "table_two"):
        operands[name] = operands[name].transpose(0, 2, 1, 3)
    operands["down"] = operands["down"].T
    for name, value in constants().items():
        operands[name] = jnp.asarray(value)
    names = tuple(operands)
    f32, b16 = jnp.float32, jnp.bfloat16
    vmem = pltpu.VMEM
    scratch = dict(
        ext=vmem((2, 4, COLUMN, D1), f32),
        rows_in=vmem((12, 12, 8, D1), f32),
        send_lon=vmem((2, 2, 224, 128), b16),
        recv_lon=vmem((2, 2, 224, 128), b16),
        send_lat=vmem((2, 2, 128, 128), b16),
        recv_lat=vmem((2, 2, 128, 128), b16),
        send_corner=vmem((2, 4, 80, 128), b16),
        recv_corner=vmem((2, 4, 80, 128), b16),
        send_all=vmem((2, 80, D2), b16),
        recv_all=vmem((2, 80, D2), b16),
        send_end=vmem((2, 2, 48, D2), b16),
        recv_end=vmem((2, 2, 2, 48, D2), b16),
        ids=vmem((6, 16, 128), b16),
        region=vmem((12, 8, 128), f32),
        table_in_one=vmem((H1, 2, PAIRS), b16),
        table_in_two=vmem((H2, 2, PAIRS), b16),
        flat_one=vmem((3, 16, TABLE), f32),
        flat_two=vmem((2, 24, TABLE), f32),
        left_one=vmem((576, 512), f32),
        left_two=vmem((576, 512), f32),
        bias_one=vmem((8, 2, 216, KEYS), f32),
        bias_two=vmem((4, 432, KEYS), f32),
        weight_kv=vmem((D1, 448), b16),
        weight_q=vmem((D1, 256), b16),
        key_mask=vmem((2, 4, COLUMN, 128), f32),
        query_mask=vmem((2, 2, COLUMN, 128), f32),
        key_mask_two=vmem((2, 2, COLUMN, 128), f32),
        query_mask_two=vmem((2, 2, COLUMN, 128), f32),
        kv=vmem((4, COLUMN, 448), f32),
        queries=vmem((2, COLUMN, 256), f32),
        heads=vmem((288, D1), f32),
        ext_two=vmem((2, 2, 144, D2), f32),
        coarse=vmem((2, 72, D2), f32),
        kv_two=vmem((2, 144, 896), f32),
        queries_two=vmem((2, 96, 512), f32),
        heads_two_out=vmem((2, 72, D2), f32),
    )
    for name in FETCHED:
        scratch["vmem_" + name] = vmem(operands[name].shape, operands[name].dtype)
    scratch["send"] = pltpu.SemaphoreType.DMA((33,))
    scratch["recv"] = pltpu.SemaphoreType.DMA((33,))
    scratch["load"] = pltpu.SemaphoreType.DMA((len(FETCHED),))
    spec = lambda name: pl.BlockSpec(memory_space=pl.ANY if name in FETCHED else vmem)
    out = pl.pallas_call(
        functools.partial(kernel, lat_size, lon_size, names, tuple(scratch)),
        out_shape=jax.ShapeDtypeStruct((6, 6, 4, D2), b16),
        in_specs=[spec(name) for name in names],
        out_specs=pl.BlockSpec(memory_space=vmem),
        scratch_shapes=list(scratch.values()),
        compiler_params=pltpu.CompilerParams(
            collective_id=0, has_side_effects=True, vmem_limit_bytes=60 * 1024 * 1024
        ),
        name="block",
    )(*operands.values())
    return out.transpose(2, 0, 1, 3)


def solution(mesh):
    split = P(None, "lat", "lon")
    table = P("lat", None, None, None)
    placed = (P(None, "lat", "lon", None), split, split) + (P(),) * 4 + (table,) + (P(),) * 8 + (table,)
    return jax.shard_map(
        functools.partial(shards, mesh.shape["lat"], mesh.shape["lon"]),
        mesh=mesh,
        in_specs=placed,
        out_specs=P(None, "lat", "lon", None),
        check_vma=False,
    )
```

```python
import functools
import types

import jax
import jax.numpy as jnp
import ml_dtypes
import numpy as np
from jax import lax
from jax.experimental import pallas as pl
from jax.experimental.pallas import tpu as pltpu
from jax.sharding import PartitionSpec as P

D1, H1, MLP = 192, 6, 768
D2, H2 = 384, 12
HEAD = 32
LIVE = 36
HELD = 48
KEYS = 4 * LIVE
COLUMN = 6 * LIVE
PAIRS = 3312
SPAN = 6 * 23
TABLE = 3456
FAR = 2.0**100
MESH = pl.DeviceIdType.MESH
LEVELS = ((1, 2), (3, 0))
TOGETHER = 8
FEATURE = 64


def atom_rows():
    return [((z * 3 + a) * 6 + o, z, a, o) for z in range(2) for a in range(3) for o in range(6)]


@functools.lru_cache(None)
def constants():
    split = np.zeros((2, 2, 40, 3, 12, 8), np.float32)
    for level in range(2):
        for og in range(2):
            for r, z, a, o in atom_rows():
                split[level, og, r, a, og * 6 + o, LEVELS[level][z]] = 1

    def spread(heads):
        rows = np.zeros((6, heads, 6, HELD), np.float32)
        for r, z, a, o in atom_rows():
            rows[o, :, z * 3 + a, r] = 1
        return rows.reshape(-1, HELD)

    def head_mask(heads, lanes):
        mask = np.zeros((6, heads, 6, lanes), np.float32)
        for h in range(heads):
            mask[:, h, :, h * HEAD : (h + 1) * HEAD] = 1
        mask[..., heads * HEAD :] = 1
        return mask.reshape(-1, lanes)

    def choose(heads, padded):
        sel = np.zeros((2, heads, 6, 6, padded), np.float32)
        for level in range(2):
            for h in range(heads):
                for za in range(6):
                    sel[level, h, za, za, 2 * h + level] = 1
        return sel.reshape(2 * heads * 6, 6 * padded)

    shift = np.zeros((2, KEYS, 512), np.float32)
    for half in range(2):
        for ah in range(2):
            for oh in range(2):
                for r, z, a, o in atom_rows():
                    lane = z * 256 + (3 * ah + a) * 23 + 6 * half - (6 * oh + o) + 11
                    shift[half, (oh * 2 + ah) * LIVE + r, lane] = 1

    repeat = np.zeros((128, 128), np.float32)
    level_lanes = np.zeros((12, 8, 128), np.float32)
    gather = np.zeros((16, 12, 8), np.float32)
    for z in range(4):
        for n in range(32):
            repeat[n, z * 32 + n] = 1
        level_lanes[:, z, z * 32 : z * 32 + 32] = 1
        for a in range(12):
            gather[a, a, z] = 1
    rows_one = np.zeros((COLUMN, 32), np.float32)
    rows_two = np.zeros((COLUMN, 32), np.float32)
    table = np.zeros((11, COLUMN, 128), np.float32)
    table[8:10, :, FEATURE : FEATURE + 4] = 1
    table[8:10, :, FEATURE + 5 : FEATURE + 25] = 1
    for ag in range(6):
        for r, z, a, o in atom_rows():
            k = ag * LIVE + r
            window, ah = ag // 2, ag % 2
            rows_one[k, (0 if window == 0 else 16) + (6, 0, 6)[window] + 3 * ah + a] = 1
            if ag < 4:
                rows_two[k, 16 * window + 3 * ah + a] = 1
            table[10, k, :] = 3 * ag + a
            for level in range(2):
                table[4 + level, k, (2 * level + z) * 32 + 16 + o] = 1
                for oh in range(2):
                    table[2 * level + oh, k, (2 * level + z) * 32 + 6 * oh + o] = 1
            for oh in range(2):
                for at in (5 + z, 7 + 3 * ah + a, 13 + 6 * oh + o):
                    table[6 + oh, k, FEATURE + at] = 1
                    table[8 + oh, k, FEATURE + at] = 0

    merge = np.zeros((4, 2, LIVE, 2, 4, LIVE), np.float32)
    for da in range(2):
        for do in range(2):
            for half in range(2):
                for r, z, a, o in atom_rows():
                    row, col = 2 * (3 * half + a) + da, 2 * o + do
                    at = (z * 3 + row % 3) * 6 + col % 6
                    merge[da * 2 + do, half, r, col // 6, row // 3, at] = 1
    final = np.zeros((6, 6, 8, 2, 2, LIVE), np.float32)
    for level in range(2):
        for half in range(2):
            for r, z, a, o in atom_rows():
                final[3 * half + a, o, LEVELS[level][z], level, half, r] = 1
    b = lambda x: x.astype(ml_dtypes.bfloat16)
    flip = lambda x: np.concatenate([x.T[:LIVE], np.zeros((4, x.shape[0]), np.float32)])
    return dict(
        split=b(split.reshape(160, 288)),
        repeat=b(repeat),
        level_lanes=level_lanes.reshape(96, 128),
        gather=b(gather.reshape(16, 96)),
        choose_one=b(choose(H1, 16)),
        choose_two=b(choose(H2, 24)),
        shift=b(shift),
        rows_one=b(rows_one),
        rows_two=b(rows_two),
        table=table,
        spread_one=b(spread(H1)),
        heads_one=b(head_mask(H1, 256)),
        turned_one=b(head_mask(H1, D1).T),
        back_one=b(flip(spread(H1))),
        merge=b(merge.reshape(288, 288)),
        spread_two=b(spread(H2)),
        heads_two=b(head_mask(H2, 512)),
        turned_two=b(head_mask(H2, D2).T),
        back_two=b(flip(spread(H2))),
        final=b(final.reshape(288, 144)),
    )


def dot(a, b):
    return jnp.dot(a, b, preferred_element_type=jnp.float32)


def dot_t(a, b):
    return lax.dot_general(a, b, (((1,), (1,)), ((), ())), preferred_element_type=jnp.float32)


def bf(x):
    return x.astype(jnp.bfloat16)


def normalize(x, gain):
    x = x.astype(jnp.float32)
    x = x - jnp.mean(x, -1, keepdims=True)
    var = jnp.mean(x * x, -1, keepdims=True)
    return bf(x * lax.rsqrt(var + 1e-5) * gain)


def attend(tasks, spread, head_mask, turned_mask, back):
    qs = [bf(dot(spread, bf(q))) * head_mask for q, _, _, _ in tasks]
    scores = [dot_t(key, q) + bias for q, (_, key, bias, _) in zip(qs, tasks)]
    weights = [jnp.exp(s - jnp.max(s, 0, keepdims=True)) for s in scores]
    probs = [bf(w * (1.0 / jnp.sum(w, 0, keepdims=True))) for w in weights]
    mixed = [bf(dot(value, p)) * turned_mask for p, (_, _, _, value) in zip(probs, tasks)]
    return [dot_t(back, m)[0:LIVE] for m in mixed]


def kernel(lat_size, lon_size, names, fetched, scratch_names, *refs):
    g = types.SimpleNamespace(**dict(zip(names, refs[: len(names)], strict=True)))
    refs = refs[len(names) :]
    g.out = refs[0]
    g.held = dict(zip(fetched, refs[1 : 1 + len(fetched)], strict=True))
    for name, ref in zip(scratch_names, refs[1 + len(fetched) :], strict=True):
        setattr(g, name, ref)
    send, recv, load = g.send, g.recv, g.load
    lat, lon = lax.axis_index("lat"), lax.axis_index("lon")
    odd = lax.rem(lon, 2)
    half_own = 1 - odd

    def at(dlat, dlon):
        return (lax.rem(lat + dlat + lat_size, lat_size), lax.rem(lon + dlon + lon_size, lon_size))

    around = [(a, o) for a in (-1, 0, 1) for o in (-1, 0, 1) if (a, o) != (0, 0)]
    barrier = pltpu.get_barrier_semaphore()
    for a, o in around + [(0, -2), (-1, -2)]:
        pl.semaphore_signal(barrier, inc=1, device_id=at(a, o), device_id_type=MESH)

    class Held:
        def __init__(self):
            self.loads = {}
            for n, name in enumerate(fetched):
                self.loads[name] = pltpu.make_async_copy(getattr(g, name), g.held[name], load.at[n])
                self.loads[name].start()

        def __getattr__(self, name):
            self.loads[name].wait()
            ref = g.held[name]
            setattr(self, name, ref)
            return ref

    v = Held()
    copies = []

    def start(src, dst, target):
        n = len(copies)
        copy = pltpu.make_async_remote_copy(
            src_ref=src, dst_ref=dst, send_sem=send.at[n], recv_sem=recv.at[n], device_id=target, device_id_type=MESH
        )
        copies.append(copy)
        copy.start()
        return copy

    ext, rows_in = g.ext, g.rows_in
    rows_in[...] = jnp.zeros_like(rows_in)
    for a in range(12):
        rows_in[a, :, 0:4, :] = v.fields[a].astype(jnp.float32)
    for ag in range(4):
        moved = dot(v.split[...], bf(rows_in[3 * ag : 3 * ag + 3].reshape(288, D1)))
        for level in range(2):
            for og in range(2):
                lo = (level * 2 + og) * 40
                ext[level, 1 + og, (1 + ag) * LIVE : (2 + ag) * LIVE, :] = moved[lo : lo + LIVE]

    def pack_level(level):
        for og in range(2):
            x = ext[level, 1 + og, LIVE : 5 * LIVE, :]
            tail = jnp.concatenate([x[0:72, 128:192], x[72:144, 128:192]], 1)
            tail = jnp.concatenate([tail, jnp.zeros((8, 128), jnp.float32)], 0)
            g.send_lon[level, og] = bf(jnp.concatenate([x[:, 0:128], tail], 0))
        for end in range(2):
            lo = (1 + 3 * end) * LIVE
            x, y = ext[level, 1, lo : lo + 40, :], ext[level, 2, lo : lo + 40, :]
            tail = jnp.concatenate([x[:, 128:192], y[:, 128:192]], 1)
            g.send_lat[level, end] = bf(
                jnp.concatenate([x[:, 0:128], y[:, 0:128], tail, jnp.zeros((8, 128), jnp.float32)], 0)
            )
            zero = jnp.zeros((40, 64), jnp.float32)
            for og, part in enumerate((x, y)):
                g.send_corner[level, 2 * end + og] = bf(
                    jnp.concatenate([part[:, 0:128], jnp.concatenate([part[:, 128:192], zero], 1)], 0)
                )

    def send_level(level):
        lon_s, lat_s, cor_s = g.send_lon, g.send_lat, g.send_corner
        lon_r, lat_r, cor_r = g.recv_lon, g.recv_lat, g.recv_corner
        return [
            start(lon_s.at[level, 0], lon_r.at[level, 1], at(0, -1)),
            start(lon_s.at[level, 1], lon_r.at[level, 0], at(0, 1)),
            start(lat_s.at[level, 0], lat_r.at[level, 1], at(-1, 0)),
            start(lat_s.at[level, 1], lat_r.at[level, 0], at(1, 0)),
            start(cor_s.at[level, 0], cor_r.at[level, 3], at(-1, -1)),
            start(cor_s.at[level, 1], cor_r.at[level, 2], at(-1, 1)),
            start(cor_s.at[level, 2], cor_r.at[level, 1], at(1, -1)),
            start(cor_s.at[level, 3], cor_r.at[level, 0], at(1, 1)),
        ]

    def unpack_level(level):
        for side in range(2):
            x = g.recv_lon[level, side].astype(jnp.float32)
            c = 3 * side
            ext[level, c, LIVE : 5 * LIVE, 0:128] = x[0:144]
            ext[level, c, LIVE : 3 * LIVE, 128:192] = x[144:216, 0:64]
            ext[level, c, 3 * LIVE : 5 * LIVE, 128:192] = x[144:216, 64:128]
            for end in range(2):
                y = g.recv_corner[level, 2 * end + side].astype(jnp.float32)
                lo = 5 * LIVE * end
                ext[level, c, lo : lo + LIVE, 0:128] = y[0:LIVE]
                ext[level, c, lo : lo + LIVE, 128:192] = y[40 : 40 + LIVE, 0:64]
        for end in range(2):
            x = g.recv_lat[level, end].astype(jnp.float32)
            lo = 5 * LIVE * end
            for og in range(2):
                ext[level, 1 + og, lo : lo + LIVE, 0:128] = x[og * 40 : og * 40 + LIVE]
                ext[level, 1 + og, lo : lo + LIVE, 128:192] = x[80 : 80 + LIVE, og * 64 : og * 64 + 64]

    pack_level(0)
    pl.semaphore_wait(barrier, 10)
    first = [send_level(0)]

    ids, region = g.ids, g.region
    region[...] = jnp.zeros_like(region)
    region[:, 0:4, 0:12] = v.region_one[...].astype(jnp.float32)
    region[0:6, 0:4, 16:22] = v.region_two[...].astype(jnp.float32)
    packed = dot(bf(region[...].reshape(96, 128)), v.repeat[...]) * v.level_lanes[...]
    ids[0] = bf(dot(v.gather[...], bf(packed)))
    id_copies = [
        start(ids.at[0], ids.at[1], at(1, 0)),
        start(ids.at[0], ids.at[2], at(0, 1)),
        start(ids.at[0], ids.at[3], at(1, 1)),
        start(ids.at[0], ids.at[4], at(0, 2)),
        start(ids.at[0], ids.at[5], at(1, 2)),
    ]
    table_copy_one = start(v.table_one.at[1], g.table_in_one, at(1, 0))
    pack_level(1)
    first.append(send_level(1))
    table_copy_two = start(v.table_two.at[0], g.table_in_two, at(1, 0))

    lane_one = lax.broadcasted_iota(jnp.int32, (D1, 256), 1)
    weight = v.project_one[...].astype(jnp.float32)
    weight_k, weight_q = g.weight_k, g.weight_q
    columns = pltpu.roll(weight[:, 128:512], 384 - 64, 1)[:, 0:256]
    weight_k[...] = bf(jnp.where(lane_one < D1, columns, 0.0))
    weight_q[...] = bf(jnp.where(lane_one < D1, weight[:, 0:256], 0.0))
    side = lax.broadcasted_iota(jnp.int32, (D2, D2), 0) == lax.broadcasted_iota(jnp.int32, (D2, D2), 1)
    eye = bf(jnp.where(side, 1.0, 0.0))
    g.turned_v_one[...] = bf(dot_t(eye[0:D1, 0:D1], bf(weight[:, 384:576])))

    def window_rows(flat, window, first_row):
        parts = []
        for zq in range(2):
            for aq in range(first_row, first_row + 3):
                pieces = []
                for zk in range(2):
                    offset = ((zq * 2 + zk) * 6 + aq) * SPAN
                    base = offset // 128 * 128
                    piece = flat[window, :, base : base + 384]
                    if offset != base:
                        piece = pltpu.roll(piece, 384 - (offset - base), 1)
                    pieces.append(piece[:, 0:256])
                parts.append(jnp.concatenate(pieces, 1))
        return bf(jnp.concatenate(parts, 0))

    def shifted(left, block, part):
        rows = part.shape[0]
        for n in range(6):
            moved = pltpu.roll(part, 512 - n, 1) if n else part
            left[block, n * rows : n * rows + rows, :] = moved

    flat_one, flat_two = g.flat_one, g.flat_two
    left_one, left_two, bias_one, bias_two = g.left_one, g.left_two, g.bias_one, g.bias_two
    flat_one[...] = jnp.zeros_like(flat_one)
    flat_two[...] = jnp.zeros_like(flat_two)

    def fill_one(ag):
        window, first_row = ((0, 3), (1, 0), (1, 3), (2, 0))[ag]
        part = dot(v.choose_one[...], window_rows(flat_one, window, first_row))
        for level in range(2):
            block = level * 4 + ag
            shifted(left_one, block, part[level * 36 : level * 36 + 36])
            left = bf(left_one[block])
            for og in range(2):
                bias_one[block, og] = dot_t(v.shift[1 - og], left)

    def fill_two(ag):
        part = dot(v.choose_two[...], window_rows(flat_two, ag, 3 - 3 * ag))
        for level in range(2):
            block = level * 2 + ag
            shifted(left_two, block, part[level * 72 : level * 72 + 72])
            bias_two[block] = dot_t(v.shift[half_own], bf(left_two[block]))

    for h in range(H1):
        for window in (1, 2):
            flat_one[window, 2 * h : 2 * h + 2, 0:PAIRS] = v.table_one[window - 1, h].astype(jnp.float32)
    for ag in (1, 2, 3):
        fill_one(ag)
    for h in range(H2):
        flat_two[1, 2 * h : 2 * h + 2, 0:PAIRS] = v.table_two[0, h].astype(jnp.float32)
    fill_two(1)
    table_copy_one.wait_recv()
    for h in range(H1):
        flat_one[0, 2 * h : 2 * h + 2, 0:PAIRS] = g.table_in_one[h].astype(jnp.float32)
    fill_one(0)

    for copy in id_copies:
        copy.wait_recv()
    table = v.table
    valid = g.valid[...]
    rows_global = valid.shape[1]
    lane_valid = lax.broadcasted_iota(jnp.int32, (COLUMN, rows_global), 1)
    lane_number = lax.broadcasted_iota(jnp.int32, (COLUMN, 128), 1).astype(jnp.float32)
    row_here = table[10, :, 0:rows_global].astype(jnp.int32)

    def wrap(row, extent):
        return jnp.where(row >= extent, row - extent, row)

    row = wrap(lax.rem(12 * lat + rows_global - 3, rows_global) + row_here, rows_global)
    alive = jnp.sum(jnp.where((lane_valid == row) & (valid == 1), 1.0, 0.0), -1, keepdims=True)
    row = wrap(lax.rem(6 * lat + rows_global // 2 - 3, rows_global // 2) + row_here, rows_global // 2)
    alive_two = jnp.max(jnp.where((lane_valid >> 1 == row) & (valid == 1), 1.0, 0.0), -1, keepdims=True)
    for side in range(2):
        mine = jnp.concatenate([ids[3 - 2 * side], ids[2 - 2 * side]], 0)
        picked = dot(v.rows_one[...], mine)
        for level in range(2):
            for oh in range(2):
                c = 2 * side + oh
                number = jnp.sum(picked * table[2 * level + oh], -1, keepdims=True)
                same = jnp.where(number + FEATURE == lane_number, 1.0, 0.0)
                g.key_mask[level, c] = same + (1.0 - alive) * table[6 + oh]
                if c in (1, 2):
                    g.query_mask[level, c - 1] = (table[8 + oh] - same) * (-FAR)
    for oh in range(2):
        slot = 2 * half_own + 2 - 2 * oh
        mine = jnp.concatenate([ids[slot + 1], ids[slot]], 0)
        picked = dot(v.rows_two[...], mine)
        for level in range(2):
            number = jnp.sum(picked * table[4 + level], -1, keepdims=True)
            same = jnp.where(number + FEATURE == lane_number, 1.0, 0.0)
            g.key_mask_two[level, oh] = same + (1.0 - alive_two) * table[6 + oh]
            g.query_mask_two[level, oh] = (table[8 + oh] - same) * (-FAR)

    queries, heads = g.queries, g.heads

    def section_one(level):
        for c in range(4):
            normed = normalize(ext[level, c], g.gain_one[...])
            g.normed_one[c] = normed.astype(jnp.float32)
            if c in (1, 2):
                q = dot(normed, weight_q[...]) * HEAD ** (-0.5)
                queries[c - 1, :, 0:128] = q[:, 0:128]
                queries[c - 1, :, 128:256] = q[:, 128:256] + g.query_mask[level, c - 1]
        places, tasks = [], []
        for side in range(2):
            for window in range(3):
                lo = window * 72
                pair = [g.normed_one[2 * side + oh, lo : lo + 72, :] for oh in range(2)]
                mask = [g.key_mask[level, 2 * side + oh, lo : lo + 72, :] for oh in range(2)]
                tokens = bf(jnp.concatenate(pair, 0))
                key = dot(tokens, weight_k[...])
                key = bf(jnp.concatenate([key[:, 0:128], key[:, 128:256] + jnp.concatenate(mask, 0)], 1))
                value = bf(dot_t(g.turned_v_one[...], tokens))
                for ah in ((1,), (0, 1), (0,))[window]:
                    ag = 2 * window + ah - 1
                    q = queries[side, (ag + 1) * LIVE : (ag + 1) * LIVE + HELD, :]
                    tasks.append((q, key, bias_one[level * 4 + ag, side], value))
                    places.append(side * 144 + ag * LIVE)
        parts = []
        for n in range(0, 8, TOGETHER):
            parts += attend(
                tasks[n : n + TOGETHER], v.spread_one[...], v.heads_one[...], v.turned_one[...], v.back_one[...]
            )
        for place, part in zip(places, parts):
            heads[place : place + LIVE] = part
        attended = bf(dot(bf(heads[...]), v.output_one[...]))
        own = jnp.concatenate([ext[level, 1 + og, LIVE : 5 * LIVE, :] for og in range(2)], 0)
        state = bf(own + attended.astype(jnp.float32))
        normed = normalize(state, g.gain_two[...])
        inner = dot(normed, v.up[...])
        inner = bf(0.5 * inner * (1.0 + lax.erf(inner * 0.5**0.5)))
        block = bf(state.astype(jnp.float32) + dot_t(inner, v.down[...]))
        parts = [dot(v.merge[n * 72 : n * 72 + 72], block) for n in range(4)]
        center = sum(jnp.sum(p, -1, keepdims=True) for p in parts) / (4 * D1)
        parts = [p - center for p in parts]
        scale = lax.rsqrt(sum(jnp.sum(p * p, -1, keepdims=True) for p in parts) / (4 * D1) + 1e-5)
        gain = g.gain_three[...].reshape(1, 4 * D1)
        coarse = sum(
            dot(bf(parts[n] * scale * gain[:, n * D1 : n * D1 + D1]), v.merge_weight[n * D1 : n * D1 + D1])
            for n in range(4)
        )
        coarse = bf(coarse).astype(jnp.float32)
        g.ext_two[level, half_own, LIVE : 3 * LIVE, :] = coarse
        g.coarse[level] = coarse
        zero = jnp.zeros((8, D2), jnp.float32)
        g.send_all[level] = bf(jnp.concatenate([coarse, zero], 0))
        g.send_end[level, 0] = bf(jnp.concatenate([coarse[0:40], zero], 0))
        g.send_end[level, 1] = bf(jnp.concatenate([coarse[32:72], zero], 0))
        to = 2 * odd - 1
        ends, into = g.send_end, g.recv_end
        return [
            start(g.send_all.at[level], g.recv_all.at[level], at(0, to)),
            start(ends.at[level, 0], into.at[level, 0, 1], at(-1, 0)),
            start(ends.at[level, 1], into.at[level, 0, 0], at(1, 0)),
            start(ends.at[level, 0], into.at[level, 1, 1], at(-1, to)),
            start(ends.at[level, 1], into.at[level, 1, 0], at(1, to)),
        ]

    def own_queries(level):
        q = dot(normalize(g.coarse[level], g.gain_four[...].reshape(1, D2)), v.project_two[:, 0:D2]) * HEAD ** (-0.5)
        g.queries_two[level, 0:72, 0:D2] = q
        g.queries_two[level, 0:72, D2:512] = g.query_mask_two[level, half_own, LIVE : 3 * LIVE, :]
        g.queries_two[level, 72:96, :] = jnp.zeros((24, 512), jnp.float32)

    heads_two, ext_two = g.heads_two_out, g.ext_two
    g.turned_v_two[...] = bf(dot_t(eye, v.project_two[:, 2 * D2 :]))

    def section_two(level):
        ext_two[level, odd, LIVE : 3 * LIVE, :] = g.recv_all[level].astype(jnp.float32)[0:72]
        for who, oh in ((0, half_own), (1, odd)):
            ext_two[level, oh, 0:LIVE, :] = g.recv_end[level, who, 0].astype(jnp.float32)[4:40]
            ext_two[level, oh, 3 * LIVE : 4 * LIVE, :] = g.recv_end[level, who, 1].astype(jnp.float32)[0:LIVE]
        for oh in range(2):
            g.normed_two[oh] = normalize(ext_two[level, oh], g.gain_four[...].reshape(1, D2)).astype(jnp.float32)
        tasks = []
        for ag in range(2):
            lo = ag * 72
            tokens = bf(jnp.concatenate([g.normed_two[oh, lo : lo + 72, :] for oh in range(2)], 0))
            mask = jnp.concatenate([g.key_mask_two[level, oh, lo : lo + 72, :] for oh in range(2)], 0)
            tasks.append(
                (
                    g.queries_two[level, ag * LIVE : ag * LIVE + HELD, :],
                    bf(jnp.concatenate([dot(tokens, v.project_two[:, D2 : 2 * D2]), mask], 1)),
                    bias_two[level * 2 + ag],
                    bf(dot_t(g.turned_v_two[...], tokens)),
                )
            )
        parts = attend(tasks, v.spread_two[...], v.heads_two[...], v.turned_two[...], v.back_two[...])
        for ag in range(2):
            heads_two[level, ag * LIVE : ag * LIVE + LIVE] = parts[ag]
        attended = bf(dot(bf(heads_two[level]), v.output_two[...]))
        return g.coarse[level] + attended.astype(jnp.float32)

    def wait_all(group):
        for copy in group:
            copy.wait_recv()

    wait_all(first[0])
    unpack_level(0)
    second = [section_one(0)]
    own_queries(0)
    wait_all(first[1])
    unpack_level(1)
    second.append(section_one(1))
    own_queries(1)

    table_copy_two.wait_recv()
    for h in range(H2):
        flat_two[0, 2 * h : 2 * h + 2, 0:PAIRS] = g.table_in_two[h].astype(jnp.float32)
    fill_two(0)

    wait_all(second[0])
    refined = [section_two(0)]
    wait_all(second[1])
    refined.append(section_two(1))
    placed = dot(v.final[...], bf(jnp.concatenate(refined, 0))).reshape(36, 8, D2)
    for i in range(6):
        g.out[i] = bf(placed[6 * i : 6 * i + 6, 0:4])
    for copy in copies:
        copy.wait_send()


def shards(
    lat_size,
    lon_size,
    fields,
    region_one,
    region_two,
    valid_rows,
    gain_one,
    project_one,
    output_one,
    table_one,
    gain_two,
    up,
    down,
    gain_three,
    merge_weight,
    gain_four,
    project_two,
    output_two,
    table_two,
):
    c = types.SimpleNamespace(**{name: jnp.asarray(value) for name, value in constants().items()})
    direct = dict(
        valid=valid_rows[None],
        gain_one=gain_one[None],
        gain_two=gain_two[None],
        gain_three=gain_three,
        gain_four=gain_four,
    )
    fetched = dict(
        fields=fields.transpose(1, 2, 0, 3),
        split=c.split,
        region_one=region_one.transpose(1, 0, 2),
        region_two=region_two.transpose(1, 0, 2),
        repeat=c.repeat,
        level_lanes=c.level_lanes,
        gather=c.gather,
        table_one=table_one.transpose(0, 2, 1, 3),
        choose_one=c.choose_one,
        shift=c.shift,
        project_one=project_one,
        rows_one=c.rows_one,
        table=c.table,
        table_two=table_two.transpose(0, 2, 1, 3),
        choose_two=c.choose_two,
        rows_two=c.rows_two,
        spread_one=c.spread_one,
        heads_one=c.heads_one,
        turned_one=c.turned_one,
        back_one=c.back_one,
        output_one=output_one,
        up=up,
        down=down.T,
        merge=c.merge,
        merge_weight=merge_weight,
        project_two=project_two,
        spread_two=c.spread_two,
        heads_two=c.heads_two,
        turned_two=c.turned_two,
        back_two=c.back_two,
        output_two=output_two,
        final=c.final,
    )
    operands = direct | fetched
    names = tuple(operands)
    f32, b16 = jnp.float32, jnp.bfloat16
    vmem = pltpu.VMEM
    scratch = dict(
        ext=vmem((2, 4, COLUMN, D1), f32),
        rows_in=vmem((12, 12, 8, D1), f32),
        send_lon=vmem((2, 2, 224, 128), b16),
        recv_lon=vmem((2, 2, 224, 128), b16),
        send_lat=vmem((2, 2, 128, 128), b16),
        recv_lat=vmem((2, 2, 128, 128), b16),
        send_corner=vmem((2, 4, 80, 128), b16),
        recv_corner=vmem((2, 4, 80, 128), b16),
        send_all=vmem((2, 80, D2), b16),
        recv_all=vmem((2, 80, D2), b16),
        send_end=vmem((2, 2, 48, D2), b16),
        recv_end=vmem((2, 2, 2, 48, D2), b16),
        ids=vmem((6, 16, 128), b16),
        region=vmem((12, 8, 128), f32),
        table_in_one=vmem((H1, 2, PAIRS), b16),
        table_in_two=vmem((H2, 2, PAIRS), b16),
        flat_one=vmem((3, 16, TABLE), f32),
        flat_two=vmem((2, 24, TABLE), f32),
        left_one=vmem((8, 216, 512), f32),
        left_two=vmem((4, 432, 512), f32),
        bias_one=vmem((8, 2, KEYS, 216), f32),
        bias_two=vmem((4, KEYS, 432), f32),
        weight_k=vmem((D1, 256), b16),
        turned_v_one=vmem((D1, D1), b16),
        turned_v_two=vmem((D2, D2), b16),
        weight_q=vmem((D1, 256), b16),
        key_mask=vmem((2, 4, COLUMN, 128), f32),
        query_mask=vmem((2, 2, COLUMN, 128), f32),
        key_mask_two=vmem((2, 2, COLUMN, 128), f32),
        query_mask_two=vmem((2, 2, COLUMN, 128), f32),
        normed_one=vmem((4, COLUMN, D1), f32),
        queries=vmem((2, COLUMN, 256), f32),
        heads=vmem((288, D1), f32),
        ext_two=vmem((2, 2, 144, D2), f32),
        coarse=vmem((2, 72, D2), f32),
        normed_two=vmem((2, 144, D2), f32),
        queries_two=vmem((2, 96, 512), f32),
        heads_two_out=vmem((2, 72, D2), f32),
    )
    held = [vmem(x.shape, x.dtype) for x in fetched.values()]
    sems = dict(
        send=pltpu.SemaphoreType.DMA((33,)),
        recv=pltpu.SemaphoreType.DMA((33,)),
        load=pltpu.SemaphoreType.DMA((len(fetched),)),
    )
    spec = lambda name: pl.BlockSpec(memory_space=pl.ANY if name in fetched else vmem)
    scratch |= sems
    out = pl.pallas_call(
        functools.partial(kernel, lat_size, lon_size, names, tuple(fetched), tuple(scratch)),
        out_shape=jax.ShapeDtypeStruct((6, 6, 4, D2), b16),
        in_specs=[spec(name) for name in names],
        out_specs=pl.BlockSpec(memory_space=vmem),
        scratch_shapes=held + list(scratch.values()),
        compiler_params=pltpu.CompilerParams(
            collective_id=0, has_side_effects=True, vmem_limit_bytes=60 * 1024 * 1024
        ),
        name="block",
    )(*operands.values())
    return out.transpose(2, 0, 1, 3)


def solution(mesh):
    split = P(None, "lat", "lon")
    table = P("lat", None, None, None)
    placed = (P(None, "lat", "lon", None), split, split) + (P(),) * 4 + (table,) + (P(),) * 8 + (table,)
    return jax.shard_map(
        functools.partial(shards, mesh.shape["lat"], mesh.shape["lon"]),
        mesh=mesh,
        in_specs=placed,
        out_specs=P(None, "lat", "lon", None),
        check_vma=False,
    )
```

```python
import functools
import types

import jax
import jax.numpy as jnp
import ml_dtypes
import numpy as np
from jax import lax
from jax.experimental import pallas as pl
from jax.experimental.pallas import tpu as pltpu
from jax.sharding import PartitionSpec as P

D1, H1, MLP = 192, 6, 768
D2, H2 = 384, 12
HEAD = 32
LIVE = 36
HELD = 48
KEYS = 4 * LIVE
COLUMN = 6 * LIVE
PAIRS = 3312
SPAN = 6 * 23
TABLE = 3456
LATER = (384, 1152, 2048, 2816)
FAR = 2.0**100
MESH = pl.DeviceIdType.MESH
LEVELS = ((1, 2), (3, 0))
TOGETHER = 8
FEATURE = 64


def atom_rows():
    return [((z * 3 + a) * 6 + o, z, a, o) for z in range(2) for a in range(3) for o in range(6)]


@functools.lru_cache(None)
def constants():
    split = np.zeros((2, 2, 40, 3, 12, 8), np.float32)
    for level in range(2):
        for og in range(2):
            for r, z, a, o in atom_rows():
                split[level, og, r, a, og * 6 + o, LEVELS[level][z]] = 1

    def spread(heads):
        rows = np.zeros((6, heads, 6, HELD), np.float32)
        for r, z, a, o in atom_rows():
            rows[o, :, z * 3 + a, r] = 1
        return rows.reshape(-1, HELD)

    def head_mask(heads, lanes):
        mask = np.zeros((6, heads, 6, lanes), np.float32)
        for h in range(heads):
            mask[:, h, :, h * HEAD : (h + 1) * HEAD] = 1
        mask[..., heads * HEAD :] = 1
        return mask.reshape(-1, lanes)

    def choose(heads, padded):
        sel = np.zeros((2, heads, 6, 6, padded), np.float32)
        for level in range(2):
            for h in range(heads):
                for za in range(6):
                    sel[level, h, za, za, 2 * h + level] = 1
        return sel.reshape(2 * heads * 6, 6 * padded)

    shift = np.zeros((2, KEYS, 512), np.float32)
    for half in range(2):
        for ah in range(2):
            for oh in range(2):
                for r, z, a, o in atom_rows():
                    lane = z * 256 + (3 * ah + a) * 23 + 6 * half - (6 * oh + o) + 11
                    shift[half, (oh * 2 + ah) * LIVE + r, lane] = 1

    repeat = np.zeros((128, 128), np.float32)
    level_lanes = np.zeros((12, 8, 128), np.float32)
    gather = np.zeros((16, 12, 8), np.float32)
    for z in range(4):
        for n in range(32):
            repeat[n, z * 32 + n] = 1
        level_lanes[:, z, z * 32 : z * 32 + 32] = 1
        for a in range(12):
            gather[a, a, z] = 1
    rows_one = np.zeros((COLUMN, 32), np.float32)
    rows_two = np.zeros((COLUMN, 32), np.float32)
    table = np.zeros((11, COLUMN, 128), np.float32)
    table[8:10, :, FEATURE : FEATURE + 4] = 1
    table[8:10, :, FEATURE + 5 : FEATURE + 25] = 1
    for ag in range(6):
        for r, z, a, o in atom_rows():
            k = ag * LIVE + r
            window, ah = ag // 2, ag % 2
            rows_one[k, (0 if window == 0 else 16) + (6, 0, 6)[window] + 3 * ah + a] = 1
            if ag < 4:
                rows_two[k, 16 * window + 3 * ah + a] = 1
            table[10, k, :] = 3 * ag + a
            for level in range(2):
                table[4 + level, k, (2 * level + z) * 32 + 16 + o] = 1
                for oh in range(2):
                    table[2 * level + oh, k, (2 * level + z) * 32 + 6 * oh + o] = 1
            for oh in range(2):
                for at in (5 + z, 7 + 3 * ah + a, 13 + 6 * oh + o):
                    table[6 + oh, k, FEATURE + at] = 1
                    table[8 + oh, k, FEATURE + at] = 0

    merge = np.zeros((4, 2, LIVE, 2, 4, LIVE), np.float32)
    for da in range(2):
        for do in range(2):
            for half in range(2):
                for r, z, a, o in atom_rows():
                    row, col = 2 * (3 * half + a) + da, 2 * o + do
                    at = (z * 3 + row % 3) * 6 + col % 6
                    merge[da * 2 + do, half, r, col // 6, row // 3, at] = 1
    final = np.zeros((6, 6, 8, 2, 2, LIVE), np.float32)
    for level in range(2):
        for half in range(2):
            for r, z, a, o in atom_rows():
                final[3 * half + a, o, LEVELS[level][z], level, half, r] = 1
    b = lambda x: x.astype(ml_dtypes.bfloat16)
    flip = lambda x: np.concatenate([x.T[:LIVE], np.zeros((4, x.shape[0]), np.float32)])
    return dict(
        split=b(split.reshape(160, 288)),
        repeat=b(repeat),
        level_lanes=level_lanes.reshape(96, 128),
        gather=b(gather.reshape(16, 96)),
        choose_one=b(choose(H1, 16)),
        choose_two=b(choose(H2, 24)),
        shift=b(shift),
        rows_one=b(rows_one),
        rows_two=b(rows_two),
        table=table,
        spread_one=b(spread(H1)),
        heads_one=b(head_mask(H1, 256)),
        turned_one=b(head_mask(H1, D1).T),
        back_one=b(flip(spread(H1))),
        merge=b(merge.reshape(288, 288)),
        spread_two=b(spread(H2)),
        heads_two=b(head_mask(H2, 512)),
        turned_two=b(head_mask(H2, D2).T),
        back_two=b(flip(spread(H2))),
        final=b(final.reshape(288, 144)),
    )


def dot(a, b):
    return jnp.dot(a, b, preferred_element_type=jnp.float32)


def dot_t(a, b):
    return lax.dot_general(a, b, (((1,), (1,)), ((), ())), preferred_element_type=jnp.float32)


def bf(x):
    return x.astype(jnp.bfloat16)


def normalize(x, gain):
    x = x.astype(jnp.float32)
    x = x - jnp.mean(x, -1, keepdims=True)
    var = jnp.mean(x * x, -1, keepdims=True)
    return bf(x * lax.rsqrt(var + 1e-5) * gain)


def attend(tasks, spread, head_mask, turned_mask, back):
    qs = [bf(dot(spread, bf(q))) * head_mask for q, _, _, _ in tasks]
    scores = [dot_t(key, q) + bias for q, (_, key, bias, _) in zip(qs, tasks)]
    weights = [jnp.exp(s - jnp.max(s, 0, keepdims=True)) for s in scores]
    probs = [bf(w * (1.0 / jnp.sum(w, 0, keepdims=True))) for w in weights]
    mixed = [bf(dot(value, p)) * turned_mask for p, (_, _, _, value) in zip(probs, tasks)]
    return [dot_t(back, m)[0:LIVE] for m in mixed]


def kernel(lat_size, lon_size, names, fetched, scratch_names, *refs):
    g = types.SimpleNamespace(**dict(zip(names, refs[: len(names)], strict=True)))
    refs = refs[len(names) :]
    g.out = refs[0]
    g.held = dict(zip(fetched, refs[1 : 1 + len(fetched)], strict=True))
    for name, ref in zip(scratch_names, refs[1 + len(fetched) :], strict=True):
        setattr(g, name, ref)
    send, recv, load = g.send, g.recv, g.load
    lat, lon = lax.axis_index("lat"), lax.axis_index("lon")
    odd = lax.rem(lon, 2)
    half_own = 1 - odd

    def at(dlat, dlon):
        return (lax.rem(lat + dlat + lat_size, lat_size), lax.rem(lon + dlon + lon_size, lon_size))

    around = [(a, o) for a in (-1, 0, 1) for o in (-1, 0, 1) if (a, o) != (0, 0)]
    barrier = pltpu.get_barrier_semaphore()
    for a, o in around + [(0, -2), (-1, -2)]:
        pl.semaphore_signal(barrier, inc=1, device_id=at(a, o), device_id_type=MESH)

    class Held:
        def __init__(self):
            self.loads = {}
            for n, name in enumerate(fetched):
                self.loads[name] = pltpu.make_async_copy(getattr(g, name), g.held[name], load.at[n])
                self.loads[name].start()

        def __getattr__(self, name):
            self.loads[name].wait()
            ref = g.held[name]
            setattr(self, name, ref)
            return ref

    v = Held()
    copies = []

    def start(src, dst, target):
        n = len(copies)
        copy = pltpu.make_async_remote_copy(
            src_ref=src, dst_ref=dst, send_sem=send.at[n], recv_sem=recv.at[n], device_id=target, device_id_type=MESH
        )
        copies.append(copy)
        copy.start()
        return copy

    ext, rows_in = g.ext, g.rows_in
    rows_in[...] = jnp.zeros_like(rows_in)
    for a in range(12):
        rows_in[a, :, 0:4, :] = v.fields[a].astype(jnp.float32)
    for ag in range(4):
        moved = dot(v.split[...], bf(rows_in[3 * ag : 3 * ag + 3].reshape(288, D1)))
        for level in range(2):
            for og in range(2):
                lo = (level * 2 + og) * 40
                ext[level, 1 + og, (1 + ag) * LIVE : (2 + ag) * LIVE, :] = moved[lo : lo + LIVE]

    g.stage[...] = jnp.zeros_like(g.stage)

    def pack_level(level):
        for og in range(2):
            x = ext[level, 1 + og, LIVE : 5 * LIVE, :]
            tail = jnp.concatenate([x[0:72, 128:192], x[72:144, 128:192]], 1)
            tail = jnp.concatenate([tail, jnp.zeros((8, 128), jnp.float32)], 0)
            g.send_lon[level, og] = bf(jnp.concatenate([x[:, 0:128], tail], 0))
        for end in range(2):
            lo = (1 + 3 * end) * LIVE
            stage = g.stage
            for og in range(2):
                stage[og * LIVE : og * LIVE + LIVE, :] = ext[level, 1 + og, lo : lo + LIVE, 0:128]
            tail = [ext[level, 1 + og, lo : lo + LIVE, 128:192] for og in range(2)]
            stage[72:108, :] = jnp.concatenate(tail, 1)
            g.send_lat[level, end] = bf(stage[...])
            for og in range(2):
                main = ext[level, 1 + og, lo : lo + 40, 0:128]
                tail = [ext[level, 1 + og, lo + n : lo + n + 24, 128:192] for n in (0, 18)]
                g.send_corner[level, 2 * end + og] = bf(jnp.concatenate([main, jnp.concatenate(tail, 1)], 0))

    def send_level(level):
        lon_s, lat_s, cor_s = g.send_lon, g.send_lat, g.send_corner
        lon_r, lat_r, cor_r = g.recv_lon, g.recv_lat, g.recv_corner
        return [
            start(lon_s.at[level, 0], lon_r.at[level, 1], at(0, -1)),
            start(lon_s.at[level, 1], lon_r.at[level, 0], at(0, 1)),
            start(lat_s.at[level, 0], lat_r.at[level, 1], at(-1, 0)),
            start(lat_s.at[level, 1], lat_r.at[level, 0], at(1, 0)),
            start(cor_s.at[level, 0], cor_r.at[level, 3], at(-1, -1)),
            start(cor_s.at[level, 1], cor_r.at[level, 2], at(-1, 1)),
            start(cor_s.at[level, 2], cor_r.at[level, 1], at(1, -1)),
            start(cor_s.at[level, 3], cor_r.at[level, 0], at(1, 1)),
        ]

    def unpack_level(level):
        for side in range(2):
            x = g.recv_lon[level, side].astype(jnp.float32)
            c = 3 * side
            ext[level, c, LIVE : 5 * LIVE, 0:128] = x[0:144]
            ext[level, c, LIVE : 3 * LIVE, 128:192] = x[144:216, 0:64]
            ext[level, c, 3 * LIVE : 5 * LIVE, 128:192] = x[144:216, 64:128]
            for end in range(2):
                y = g.recv_corner[level, 2 * end + side].astype(jnp.float32)
                lo = 5 * LIVE * end
                ext[level, c, lo : lo + LIVE, 0:128] = y[0:LIVE]
                for n in range(2):
                    ext[level, c, lo + 18 * n : lo + 18 * n + 18, 128:192] = y[40:58, 64 * n : 64 * n + 64]
        for end in range(2):
            x = g.recv_lat[level, end].astype(jnp.float32)
            lo = 5 * LIVE * end
            for og in range(2):
                ext[level, 1 + og, lo : lo + LIVE, 0:128] = x[og * LIVE : og * LIVE + LIVE]
                ext[level, 1 + og, lo : lo + LIVE, 128:192] = x[72:108, og * 64 : og * 64 + 64]

    pack_level(0)
    pl.semaphore_wait(barrier, 10)
    first = [send_level(0)]

    ids, region = g.ids, g.region
    region[...] = jnp.zeros_like(region)
    region[:, 0:4, 0:12] = v.region_one[...].astype(jnp.float32)
    region[0:6, 0:4, 16:22] = v.region_two[...].astype(jnp.float32)
    packed = dot(bf(region[...].reshape(96, 128)), v.repeat[...]) * v.level_lanes[...]
    ids[0] = bf(dot(v.gather[...], bf(packed)))
    id_copies = [
        start(ids.at[0], ids.at[1], at(1, 0)),
        start(ids.at[0], ids.at[2], at(0, 1)),
        start(ids.at[0], ids.at[3], at(1, 1)),
        start(ids.at[0], ids.at[4], at(0, 2)),
        start(ids.at[0], ids.at[5], at(1, 2)),
    ]
    def pack_table(table, which, heads, packed):
        packed[...] = jnp.zeros_like(packed)
        for n, lane in enumerate(LATER):
            wide = min(512, PAIRS - lane)
            packed[n, :, :, 0:wide] = table[which, pl.ds(heads * odd, heads), :, lane : lane + wide]

    def unpack_table(flat, tables, heads):
        for half in range(2):
            for n, lane in enumerate(LATER):
                for h in range(heads):
                    row = 2 * (half * heads + h)
                    flat[0, row : row + 2, lane : lane + 512] = tables[half, n, h].astype(jnp.float32)

    def to_other_core(tables):
        return start(tables.at[odd], tables.at[odd], at(0, 1 - 2 * odd))

    pack_table(v.table_one, 1, H1 // 2, g.table_out_one)
    table_copy_one = start(g.table_out_one, g.table_in_one.at[odd], at(1, 0))
    pack_level(1)
    first.append(send_level(1))
    pack_table(v.table_two, 0, H2 // 2, g.table_out_two)
    table_copy_two = start(g.table_out_two, g.table_in_two.at[odd], at(1, 0))

    lane_one = lax.broadcasted_iota(jnp.int32, (D1, 256), 1)
    weight = v.project_one[...].astype(jnp.float32)
    weight_k, weight_q = g.weight_k, g.weight_q
    columns = pltpu.roll(weight[:, 128:512], 384 - 64, 1)[:, 0:256]
    weight_k[...] = bf(jnp.where(lane_one < D1, columns, 0.0))
    weight_q[...] = bf(jnp.where(lane_one < D1, weight[:, 0:256], 0.0))
    side = lax.broadcasted_iota(jnp.int32, (D2, D2), 0) == lax.broadcasted_iota(jnp.int32, (D2, D2), 1)
    eye = bf(jnp.where(side, 1.0, 0.0))
    g.turned_v_one[...] = bf(dot_t(eye[0:D1, 0:D1], bf(weight[:, 384:576])))

    def window_rows(flat, window, first_row):
        parts = []
        for zq in range(2):
            for aq in range(first_row, first_row + 3):
                pieces = []
                for zk in range(2):
                    offset = ((zq * 2 + zk) * 6 + aq) * SPAN
                    base = offset // 128 * 128
                    piece = flat[window, :, base : base + 384]
                    if offset != base:
                        piece = pltpu.roll(piece, 384 - (offset - base), 1)
                    pieces.append(piece[:, 0:256])
                parts.append(jnp.concatenate(pieces, 1))
        return bf(jnp.concatenate(parts, 0))

    def shifted(left, block, part):
        rows = part.shape[0]
        for n in range(6):
            moved = pltpu.roll(part, 512 - n, 1) if n else part
            left[block, n * rows : n * rows + rows, :] = moved

    flat_one, flat_two = g.flat_one, g.flat_two
    left_one, left_two, bias_one, bias_two = g.left_one, g.left_two, g.bias_one, g.bias_two
    flat_one[...] = jnp.zeros_like(flat_one)
    flat_two[...] = jnp.zeros_like(flat_two)

    def fill_one(ag):
        window, first_row = ((0, 3), (1, 0), (1, 3), (2, 0))[ag]
        part = dot(v.choose_one[...], window_rows(flat_one, window, first_row))
        for level in range(2):
            block = level * 4 + ag
            shifted(left_one, block, part[level * 36 : level * 36 + 36])
            left = bf(left_one[block])
            for og in range(2):
                bias_one[block, og] = dot_t(v.shift[1 - og], left)

    def fill_two(ag):
        part = dot(v.choose_two[...], window_rows(flat_two, ag, 3 - 3 * ag))
        for level in range(2):
            block = level * 2 + ag
            shifted(left_two, block, part[level * 72 : level * 72 + 72])
            bias_two[block] = dot_t(v.shift[half_own], bf(left_two[block]))

    for h in range(H1):
        for window in (1, 2):
            flat_one[window, 2 * h : 2 * h + 2, 0:PAIRS] = v.table_one[window - 1, h].astype(jnp.float32)
    for ag in (1, 2, 3):
        fill_one(ag)
    for h in range(H2):
        flat_two[1, 2 * h : 2 * h + 2, 0:PAIRS] = v.table_two[0, h].astype(jnp.float32)
    fill_two(1)
    table_copy_one.wait_recv()
    table_copy_one = to_other_core(g.table_in_one)

    for copy in id_copies:
        copy.wait_recv()
    table = v.table
    valid = g.valid[...]
    rows_global = valid.shape[1]
    lane_valid = lax.broadcasted_iota(jnp.int32, (COLUMN, rows_global), 1)
    lane_number = lax.broadcasted_iota(jnp.int32, (COLUMN, 128), 1).astype(jnp.float32)
    row_here = table[10, :, 0:rows_global].astype(jnp.int32)

    def wrap(row, extent):
        return jnp.where(row >= extent, row - extent, row)

    row = wrap(lax.rem(12 * lat + rows_global - 3, rows_global) + row_here, rows_global)
    alive = jnp.sum(jnp.where((lane_valid == row) & (valid == 1), 1.0, 0.0), -1, keepdims=True)
    row = wrap(lax.rem(6 * lat + rows_global // 2 - 3, rows_global // 2) + row_here, rows_global // 2)
    alive_two = jnp.max(jnp.where((lane_valid >> 1 == row) & (valid == 1), 1.0, 0.0), -1, keepdims=True)
    for side in range(2):
        mine = jnp.concatenate([ids[3 - 2 * side], ids[2 - 2 * side]], 0)
        picked = dot(v.rows_one[...], mine)
        for level in range(2):
            for oh in range(2):
                c = 2 * side + oh
                number = jnp.sum(picked * table[2 * level + oh], -1, keepdims=True)
                same = jnp.where(number + FEATURE == lane_number, 1.0, 0.0)
                g.key_mask[level, c] = same + (1.0 - alive) * table[6 + oh]
                if c in (1, 2):
                    g.query_mask[level, c - 1] = (table[8 + oh] - same) * (-FAR)
    for oh in range(2):
        slot = 2 * half_own + 2 - 2 * oh
        mine = jnp.concatenate([ids[slot + 1], ids[slot]], 0)
        picked = dot(v.rows_two[...], mine)
        for level in range(2):
            number = jnp.sum(picked * table[4 + level], -1, keepdims=True)
            same = jnp.where(number + FEATURE == lane_number, 1.0, 0.0)
            g.key_mask_two[level, oh] = same + (1.0 - alive_two) * table[6 + oh]
            g.query_mask_two[level, oh] = (table[8 + oh] - same) * (-FAR)

    table_copy_one.wait_recv()
    unpack_table(flat_one, g.table_in_one, H1 // 2)
    fill_one(0)

    queries, heads = g.queries, g.heads

    def section_one(level):
        for c in range(4):
            normed = normalize(ext[level, c], g.gain_one[...])
            g.normed_one[c] = normed.astype(jnp.float32)
            if c in (1, 2):
                q = dot(normed, weight_q[...]) * HEAD ** (-0.5)
                queries[c - 1, :, 0:128] = q[:, 0:128]
                queries[c - 1, :, 128:256] = q[:, 128:256] + g.query_mask[level, c - 1]
        places, tasks = [], []
        for side in range(2):
            for window in range(3):
                lo = window * 72
                pair = [g.normed_one[2 * side + oh, lo : lo + 72, :] for oh in range(2)]
                mask = [g.key_mask[level, 2 * side + oh, lo : lo + 72, :] for oh in range(2)]
                tokens = bf(jnp.concatenate(pair, 0))
                key = dot(tokens, weight_k[...])
                key = bf(jnp.concatenate([key[:, 0:128], key[:, 128:256] + jnp.concatenate(mask, 0)], 1))
                value = bf(dot_t(g.turned_v_one[...], tokens))
                for ah in ((1,), (0, 1), (0,))[window]:
                    ag = 2 * window + ah - 1
                    q = queries[side, (ag + 1) * LIVE : (ag + 1) * LIVE + HELD, :]
                    tasks.append((q, key, bias_one[level * 4 + ag, side], value))
                    places.append(side * 144 + ag * LIVE)
        parts = []
        for n in range(0, 8, TOGETHER):
            parts += attend(
                tasks[n : n + TOGETHER], v.spread_one[...], v.heads_one[...], v.turned_one[...], v.back_one[...]
            )
        for place, part in zip(places, parts):
            heads[place : place + LIVE] = part
        attended = bf(dot(bf(heads[...]), v.output_one[...]))
        own = jnp.concatenate([ext[level, 1 + og, LIVE : 5 * LIVE, :] for og in range(2)], 0)
        state = bf(own + attended.astype(jnp.float32))
        normed = normalize(state, g.gain_two[...])
        inner = dot(normed, v.up[...])
        inner = bf(0.5 * inner * (1.0 + lax.erf(inner * 0.5**0.5)))
        block = bf(state.astype(jnp.float32) + dot_t(inner, v.down[...]))
        parts = dot(v.merge[...], block)
        parts = [parts[n * 72 : n * 72 + 72] for n in range(4)]
        center = sum(jnp.sum(p, -1, keepdims=True) for p in parts) / (4 * D1)
        parts = [p - center for p in parts]
        scale = lax.rsqrt(sum(jnp.sum(p * p, -1, keepdims=True) for p in parts) / (4 * D1) + 1e-5)
        gain = g.gain_three[...].reshape(1, 4 * D1)
        coarse = sum(
            dot(bf(parts[n] * scale * gain[:, n * D1 : n * D1 + D1]), v.merge_weight[n * D1 : n * D1 + D1])
            for n in range(4)
        )
        coarse = bf(coarse).astype(jnp.float32)
        g.ext_two[level, half_own, LIVE : 3 * LIVE, :] = coarse
        g.coarse[level] = coarse
        zero = jnp.zeros((8, D2), jnp.float32)
        g.send_all[level] = bf(jnp.concatenate([coarse, zero], 0))
        g.send_end[level, 0] = bf(jnp.concatenate([coarse[0:40], zero], 0))
        g.send_end[level, 1] = bf(jnp.concatenate([coarse[32:72], zero], 0))
        to = 2 * odd - 1
        ends, into = g.send_end, g.recv_end
        return [
            start(g.send_all.at[level], g.recv_all.at[level], at(0, to)),
            start(ends.at[level, 0], into.at[level, 0, 1], at(-1, 0)),
            start(ends.at[level, 1], into.at[level, 0, 0], at(1, 0)),
            start(ends.at[level, 0], into.at[level, 1, 1], at(-1, to)),
            start(ends.at[level, 1], into.at[level, 1, 0], at(1, to)),
        ]

    def own_queries(level):
        q = dot(normalize(g.coarse[level], g.gain_four[...].reshape(1, D2)), v.project_two[:, 0:D2]) * HEAD ** (-0.5)
        g.queries_two[level, 0:72, 0:D2] = q
        g.queries_two[level, 0:72, D2:512] = g.query_mask_two[level, half_own, LIVE : 3 * LIVE, :]
        g.queries_two[level, 72:96, :] = jnp.zeros((24, 512), jnp.float32)

    heads_two, ext_two = g.heads_two_out, g.ext_two
    g.turned_v_two[...] = bf(dot_t(eye, v.project_two[:, 2 * D2 :]))

    def section_two(level):
        ext_two[level, odd, LIVE : 3 * LIVE, :] = g.recv_all[level].astype(jnp.float32)[0:72]
        for who, oh in ((0, half_own), (1, odd)):
            ext_two[level, oh, 0:LIVE, :] = g.recv_end[level, who, 0].astype(jnp.float32)[4:40]
            ext_two[level, oh, 3 * LIVE : 4 * LIVE, :] = g.recv_end[level, who, 1].astype(jnp.float32)[0:LIVE]
        for oh in range(2):
            g.normed_two[oh] = normalize(ext_two[level, oh], g.gain_four[...].reshape(1, D2)).astype(jnp.float32)
        tasks = []
        for ag in range(2):
            lo = ag * 72
            tokens = bf(jnp.concatenate([g.normed_two[oh, lo : lo + 72, :] for oh in range(2)], 0))
            mask = jnp.concatenate([g.key_mask_two[level, oh, lo : lo + 72, :] for oh in range(2)], 0)
            tasks.append(
                (
                    g.queries_two[level, ag * LIVE : ag * LIVE + HELD, :],
                    bf(jnp.concatenate([dot(tokens, v.project_two[:, D2 : 2 * D2]), mask], 1)),
                    bias_two[level * 2 + ag],
                    bf(dot_t(g.turned_v_two[...], tokens)),
                )
            )
        parts = attend(tasks, v.spread_two[...], v.heads_two[...], v.turned_two[...], v.back_two[...])
        for ag in range(2):
            heads_two[level, ag * LIVE : ag * LIVE + LIVE] = parts[ag]
        attended = bf(dot(bf(heads_two[level]), v.output_two[...]))
        return g.coarse[level] + attended.astype(jnp.float32)

    def wait_all(group):
        for copy in group:
            copy.wait_recv()

    wait_all(first[0])
    unpack_level(0)
    second = [section_one(0)]
    own_queries(0)
    wait_all(first[1])
    table_copy_two.wait_recv()
    table_copy_two = to_other_core(g.table_in_two)
    unpack_level(1)
    second.append(section_one(1))
    own_queries(1)

    table_copy_two.wait_recv()
    unpack_table(flat_two, g.table_in_two, H2 // 2)
    fill_two(0)

    wait_all(second[0])
    refined = [section_two(0)]
    wait_all(second[1])
    refined.append(section_two(1))
    placed = dot(v.final[...], bf(jnp.concatenate(refined, 0))).reshape(36, 8, D2)
    for i in range(6):
        g.out[i] = bf(placed[6 * i : 6 * i + 6, 0:4])
    for copy in copies:
        copy.wait_send()


def shards(
    lat_size,
    lon_size,
    fields,
    region_one,
    region_two,
    valid_rows,
    gain_one,
    project_one,
    output_one,
    table_one,
    gain_two,
    up,
    down,
    gain_three,
    merge_weight,
    gain_four,
    project_two,
    output_two,
    table_two,
):
    c = types.SimpleNamespace(**{name: jnp.asarray(value) for name, value in constants().items()})
    direct = dict(
        valid=valid_rows[None],
        gain_one=gain_one[None],
        gain_two=gain_two[None],
        gain_three=gain_three,
        gain_four=gain_four,
    )
    fetched = dict(
        fields=fields.transpose(1, 2, 0, 3),
        split=c.split,
        region_one=region_one.transpose(1, 0, 2),
        region_two=region_two.transpose(1, 0, 2),
        repeat=c.repeat,
        level_lanes=c.level_lanes,
        gather=c.gather,
        table_one=table_one.transpose(0, 2, 1, 3),
        choose_one=c.choose_one,
        shift=c.shift,
        project_one=project_one,
        rows_one=c.rows_one,
        table=c.table,
        table_two=table_two.transpose(0, 2, 1, 3),
        choose_two=c.choose_two,
        rows_two=c.rows_two,
        spread_one=c.spread_one,
        heads_one=c.heads_one,
        turned_one=c.turned_one,
        back_one=c.back_one,
        output_one=output_one,
        up=up,
        down=down.T,
        merge=c.merge,
        merge_weight=merge_weight,
        project_two=project_two,
        spread_two=c.spread_two,
        heads_two=c.heads_two,
        turned_two=c.turned_two,
        back_two=c.back_two,
        output_two=output_two,
        final=c.final,
    )
    operands = direct | fetched
    names = tuple(operands)
    f32, b16 = jnp.float32, jnp.bfloat16
    vmem = pltpu.VMEM
    scratch = dict(
        ext=vmem((2, 4, COLUMN, D1), f32),
        rows_in=vmem((12, 12, 8, D1), f32),
        send_lon=vmem((2, 2, 224, 128), b16),
        recv_lon=vmem((2, 2, 224, 128), b16),
        stage=vmem((112, 128), f32),
        send_lat=vmem((2, 2, 112, 128), b16),
        recv_lat=vmem((2, 2, 112, 128), b16),
        send_corner=vmem((2, 4, 64, 128), b16),
        recv_corner=vmem((2, 4, 64, 128), b16),
        send_all=vmem((2, 80, D2), b16),
        recv_all=vmem((2, 80, D2), b16),
        send_end=vmem((2, 2, 48, D2), b16),
        recv_end=vmem((2, 2, 2, 48, D2), b16),
        ids=vmem((6, 16, 128), b16),
        region=vmem((12, 8, 128), f32),
        table_out_one=vmem((4, H1 // 2, 2, 512), b16),
        table_out_two=vmem((4, H2 // 2, 2, 512), b16),
        table_in_one=vmem((2, 4, H1 // 2, 2, 512), b16),
        table_in_two=vmem((2, 4, H2 // 2, 2, 512), b16),
        flat_one=vmem((3, 16, TABLE), f32),
        flat_two=vmem((2, 24, TABLE), f32),
        left_one=vmem((8, 216, 512), f32),
        left_two=vmem((4, 432, 512), f32),
        bias_one=vmem((8, 2, KEYS, 216), f32),
        bias_two=vmem((4, KEYS, 432), f32),
        weight_k=vmem((D1, 256), b16),
        turned_v_one=vmem((D1, D1), b16),
        turned_v_two=vmem((D2, D2), b16),
        weight_q=vmem((D1, 256), b16),
        key_mask=vmem((2, 4, COLUMN, 128), f32),
        query_mask=vmem((2, 2, COLUMN, 128), f32),
        key_mask_two=vmem((2, 2, COLUMN, 128), f32),
        query_mask_two=vmem((2, 2, COLUMN, 128), f32),
        normed_one=vmem((4, COLUMN, D1), f32),
        queries=vmem((2, COLUMN, 256), f32),
        heads=vmem((288, D1), f32),
        ext_two=vmem((2, 2, 144, D2), f32),
        coarse=vmem((2, 72, D2), f32),
        normed_two=vmem((2, 144, D2), f32),
        queries_two=vmem((2, 96, 512), f32),
        heads_two_out=vmem((2, 72, D2), f32),
    )
    held = [vmem(x.shape, x.dtype) for x in fetched.values()]
    sems = dict(
        send=pltpu.SemaphoreType.DMA((35,)),
        recv=pltpu.SemaphoreType.DMA((35,)),
        load=pltpu.SemaphoreType.DMA((len(fetched),)),
    )
    spec = lambda name: pl.BlockSpec(memory_space=pl.ANY if name in fetched else vmem)
    scratch |= sems
    out = pl.pallas_call(
        functools.partial(kernel, lat_size, lon_size, names, tuple(fetched), tuple(scratch)),
        out_shape=jax.ShapeDtypeStruct((6, 6, 4, D2), b16),
        in_specs=[spec(name) for name in names],
        out_specs=pl.BlockSpec(memory_space=vmem),
        scratch_shapes=held + list(scratch.values()),
        compiler_params=pltpu.CompilerParams(
            collective_id=0, has_side_effects=True, vmem_limit_bytes=60 * 1024 * 1024
        ),
        name="block",
    )(*operands.values())
    return out.transpose(2, 0, 1, 3)


def solution(mesh):
    split = P(None, "lat", "lon")
    table = P("lat", None, None, None)
    placed = (P(None, "lat", "lon", None), split, split) + (P(),) * 4 + (table,) + (P(),) * 8 + (table,)
    return jax.shard_map(
        functools.partial(shards, mesh.shape["lat"], mesh.shape["lon"]),
        mesh=mesh,
        in_specs=placed,
        out_specs=P(None, "lat", "lon", None),
        check_vma=False,
    )
```

```python
import functools
import types

import jax
import jax.numpy as jnp
import ml_dtypes
import numpy as np
from jax import lax
from jax.experimental import pallas as pl
from jax.experimental.pallas import tpu as pltpu
from jax.sharding import PartitionSpec as P

D1, H1, MLP = 192, 6, 768
D2, H2 = 384, 12
HEAD = 32
LIVE = 36
HELD = 48
KEYS = 4 * LIVE
COLUMN = 6 * LIVE
PAIRS = 3312
SPAN = 6 * 23
TABLE = 3456
LATER = (384, 1152, 2048, 2816)
FAR = 2.0**100
MESH = pl.DeviceIdType.MESH
LEVELS = ((1, 2), (3, 0))
TOGETHER = 8
FEATURE = 64


def atom_rows():
    return [((z * 3 + a) * 6 + o, z, a, o) for z in range(2) for a in range(3) for o in range(6)]


@functools.lru_cache(None)
def constants():
    split = np.zeros((2, 2, 40, 3, 12, 8), np.float32)
    for level in range(2):
        for og in range(2):
            for r, z, a, o in atom_rows():
                split[level, og, r, a, og * 6 + o, LEVELS[level][z]] = 1

    def spread(heads):
        rows = np.zeros((6, heads, 6, HELD), np.float32)
        for r, z, a, o in atom_rows():
            rows[o, :, z * 3 + a, r] = 1
        return rows.reshape(-1, HELD)

    def head_mask(heads, lanes):
        mask = np.zeros((6, heads, 6, lanes), np.float32)
        for h in range(heads):
            mask[:, h, :, h * HEAD : (h + 1) * HEAD] = 1
        mask[..., heads * HEAD :] = 1
        return mask.reshape(-1, lanes)

    def choose(heads, padded):
        sel = np.zeros((2, heads, 6, 6, padded), np.float32)
        for level in range(2):
            for h in range(heads):
                for za in range(6):
                    sel[level, h, za, za, 2 * h + level] = 1
        return sel.reshape(2 * heads * 6, 6 * padded)

    shift = np.zeros((2, KEYS, 512), np.float32)
    for half in range(2):
        for ah in range(2):
            for oh in range(2):
                for r, z, a, o in atom_rows():
                    lane = z * 256 + (3 * ah + a) * 23 + 6 * half - (6 * oh + o) + 11
                    shift[half, (oh * 2 + ah) * LIVE + r, lane] = 1

    repeat = np.zeros((128, 128), np.float32)
    level_lanes = np.zeros((12, 8, 128), np.float32)
    gather = np.zeros((16, 12, 8), np.float32)
    for z in range(4):
        for n in range(32):
            repeat[n, z * 32 + n] = 1
        level_lanes[:, z, z * 32 : z * 32 + 32] = 1
        for a in range(12):
            gather[a, a, z] = 1
    rows_one = np.zeros((COLUMN, 32), np.float32)
    rows_two = np.zeros((COLUMN, 32), np.float32)
    table = np.zeros((11, COLUMN, 128), np.float32)
    table[8:10, :, FEATURE : FEATURE + 4] = 1
    table[8:10, :, FEATURE + 5 : FEATURE + 25] = 1
    for ag in range(6):
        for r, z, a, o in atom_rows():
            k = ag * LIVE + r
            window, ah = ag // 2, ag % 2
            rows_one[k, (0 if window == 0 else 16) + (6, 0, 6)[window] + 3 * ah + a] = 1
            if ag < 4:
                rows_two[k, 16 * window + 3 * ah + a] = 1
            table[10, k, :] = 3 * ag + a
            for level in range(2):
                table[4 + level, k, (2 * level + z) * 32 + 16 + o] = 1
                for oh in range(2):
                    table[2 * level + oh, k, (2 * level + z) * 32 + 6 * oh + o] = 1
            for oh in range(2):
                for at in (5 + z, 7 + 3 * ah + a, 13 + 6 * oh + o):
                    table[6 + oh, k, FEATURE + at] = 1
                    table[8 + oh, k, FEATURE + at] = 0

    merge = np.zeros((4, 2, LIVE, 2, 4, LIVE), np.float32)
    for da in range(2):
        for do in range(2):
            for half in range(2):
                for r, z, a, o in atom_rows():
                    row, col = 2 * (3 * half + a) + da, 2 * o + do
                    at = (z * 3 + row % 3) * 6 + col % 6
                    merge[da * 2 + do, half, r, col // 6, row // 3, at] = 1
    final = np.zeros((6, 6, 8, 2, 2, LIVE), np.float32)
    for level in range(2):
        for half in range(2):
            for r, z, a, o in atom_rows():
                final[3 * half + a, o, LEVELS[level][z], level, half, r] = 1
    b = lambda x: x.astype(ml_dtypes.bfloat16)
    flip = lambda x: np.concatenate([x.T[:LIVE], np.zeros((4, x.shape[0]), np.float32)])
    return dict(
        split=b(split.reshape(160, 288)),
        repeat=b(repeat),
        level_lanes=level_lanes.reshape(96, 128),
        gather=b(gather.reshape(16, 96)),
        choose_one=b(choose(H1, 16)),
        choose_two=b(choose(H2, 24)),
        shift=b(shift),
        rows_one=b(rows_one),
        rows_two=b(rows_two),
        table=table,
        spread_one=b(spread(H1)),
        heads_one=b(head_mask(H1, 256)),
        turned_one=b(head_mask(H1, D1).T),
        back_one=b(flip(spread(H1))),
        merge=b(merge.reshape(288, 288)),
        spread_two=b(spread(H2)),
        heads_two=b(head_mask(H2, 512)),
        turned_two=b(head_mask(H2, D2).T),
        back_two=b(flip(spread(H2))),
        final=b(final.reshape(288, 144)),
    )


def dot(a, b):
    return jnp.dot(a, b, preferred_element_type=jnp.float32)


def dot_t(a, b):
    return lax.dot_general(a, b, (((1,), (1,)), ((), ())), preferred_element_type=jnp.float32)


def bf(x):
    return x.astype(jnp.bfloat16)


def normalize(x, gain):
    x = x.astype(jnp.float32)
    x = x - jnp.mean(x, -1, keepdims=True)
    var = jnp.mean(x * x, -1, keepdims=True)
    return bf(x * lax.rsqrt(var + 1e-5) * gain)


def attend(tasks, spread, head_mask, turned_mask, back):
    qs = [bf(dot(spread, bf(q))) * head_mask for q, _, _, _ in tasks]
    scores = [dot_t(key, q) + bias for q, (_, key, bias, _) in zip(qs, tasks)]
    weights = [jnp.exp(s - jnp.max(s, 0, keepdims=True)) for s in scores]
    probs = [bf(w * (1.0 / jnp.sum(w, 0, keepdims=True))) for w in weights]
    mixed = [bf(dot(value, p)) * turned_mask for p, (_, _, _, value) in zip(probs, tasks)]
    return [dot_t(back, m)[0:LIVE] for m in mixed]


def kernel(lat_size, lon_size, names, fetched, scratch_names, *refs):
    g = types.SimpleNamespace(**dict(zip(names, refs[: len(names)], strict=True)))
    refs = refs[len(names) :]
    g.out = refs[0]
    g.held = dict(zip(fetched, refs[1 : 1 + len(fetched)], strict=True))
    for name, ref in zip(scratch_names, refs[1 + len(fetched) :], strict=True):
        setattr(g, name, ref)
    send, recv, load = g.send, g.recv, g.load
    lat, lon = lax.axis_index("lat"), lax.axis_index("lon")
    odd = lax.rem(lon, 2)
    half_own = 1 - odd

    def at(dlat, dlon):
        return (lax.rem(lat + dlat + lat_size, lat_size), lax.rem(lon + dlon + lon_size, lon_size))

    around = [(a, o) for a in (-1, 0, 1) for o in (-1, 0, 1) if (a, o) != (0, 0)]
    barrier = pltpu.get_barrier_semaphore()
    for a, o in around + [(0, -2), (-1, -2)]:
        pl.semaphore_signal(barrier, inc=1, device_id=at(a, o), device_id_type=MESH)

    class Held:
        def __init__(self):
            self.loads = {}
            for n, name in enumerate(fetched):
                self.loads[name] = pltpu.make_async_copy(getattr(g, name), g.held[name], load.at[n])
                self.loads[name].start()

        def __getattr__(self, name):
            self.loads[name].wait()
            ref = g.held[name]
            setattr(self, name, ref)
            return ref

    v = Held()
    copies = []

    def start(src, dst, target):
        n = len(copies)
        copy = pltpu.make_async_remote_copy(
            src_ref=src, dst_ref=dst, send_sem=send.at[n], recv_sem=recv.at[n], device_id=target, device_id_type=MESH
        )
        copies.append(copy)
        copy.start()
        return copy

    ext, rows_in = g.ext, g.rows_in
    rows_in[...] = jnp.zeros_like(rows_in)
    for a in range(12):
        rows_in[a, :, 0:4, :] = v.fields[a].astype(jnp.float32)
    for ag in range(4):
        moved = dot(v.split[...], bf(rows_in[3 * ag : 3 * ag + 3].reshape(288, D1)))
        for level in range(2):
            for og in range(2):
                lo = (level * 2 + og) * 40
                ext[level, 1 + og, (1 + ag) * LIVE : (2 + ag) * LIVE, :] = moved[lo : lo + LIVE]

    g.stage[...] = jnp.zeros_like(g.stage)

    def pack_level(level):
        for og in range(2):
            x = ext[level, 1 + og, LIVE : 5 * LIVE, :]
            tail = jnp.concatenate([x[0:72, 128:192], x[72:144, 128:192]], 1)
            tail = jnp.concatenate([tail, jnp.zeros((8, 128), jnp.float32)], 0)
            g.send_lon[level, og] = bf(jnp.concatenate([x[:, 0:128], tail], 0))
        for end in range(2):
            lo = (1 + 3 * end) * LIVE
            stage = g.stage
            for og in range(2):
                stage[og * LIVE : og * LIVE + LIVE, :] = ext[level, 1 + og, lo : lo + LIVE, 0:128]
            tail = [ext[level, 1 + og, lo : lo + LIVE, 128:192] for og in range(2)]
            stage[72:108, :] = jnp.concatenate(tail, 1)
            g.send_lat[level, end] = bf(stage[...])
            for og in range(2):
                main = ext[level, 1 + og, lo : lo + 40, 0:128]
                tail = [ext[level, 1 + og, lo + n : lo + n + 24, 128:192] for n in (0, 18)]
                g.send_corner[level, 2 * end + og] = bf(jnp.concatenate([main, jnp.concatenate(tail, 1)], 0))

    def send_level(level):
        lon_s, lat_s, cor_s = g.send_lon, g.send_lat, g.send_corner
        lon_r, lat_r, cor_r = g.recv_lon, g.recv_lat, g.recv_corner
        return [
            start(lat_s.at[level, 0], lat_r.at[level, 1], at(-1, 0)),
            start(lat_s.at[level, 1], lat_r.at[level, 0], at(1, 0)),
            start(lon_s.at[level, 0], lon_r.at[level, 1], at(0, -1)),
            start(lon_s.at[level, 1], lon_r.at[level, 0], at(0, 1)),
            start(cor_s.at[level, 0], cor_r.at[level, 3], at(-1, -1)),
            start(cor_s.at[level, 1], cor_r.at[level, 2], at(-1, 1)),
            start(cor_s.at[level, 2], cor_r.at[level, 1], at(1, -1)),
            start(cor_s.at[level, 3], cor_r.at[level, 0], at(1, 1)),
        ]

    def unpack_level(level):
        for side in range(2):
            x = g.recv_lon[level, side].astype(jnp.float32)
            c = 3 * side
            ext[level, c, LIVE : 5 * LIVE, 0:128] = x[0:144]
            ext[level, c, LIVE : 3 * LIVE, 128:192] = x[144:216, 0:64]
            ext[level, c, 3 * LIVE : 5 * LIVE, 128:192] = x[144:216, 64:128]
            for end in range(2):
                y = g.recv_corner[level, 2 * end + side].astype(jnp.float32)
                lo = 5 * LIVE * end
                ext[level, c, lo : lo + LIVE, 0:128] = y[0:LIVE]
                for n in range(2):
                    ext[level, c, lo + 18 * n : lo + 18 * n + 18, 128:192] = y[40:58, 64 * n : 64 * n + 64]
        for end in range(2):
            x = g.recv_lat[level, end].astype(jnp.float32)
            lo = 5 * LIVE * end
            for og in range(2):
                ext[level, 1 + og, lo : lo + LIVE, 0:128] = x[og * LIVE : og * LIVE + LIVE]
                ext[level, 1 + og, lo : lo + LIVE, 128:192] = x[72:108, og * 64 : og * 64 + 64]

    pack_level(0)
    pl.semaphore_wait(barrier, 10)
    first = [send_level(0)]

    ids, region = g.ids, g.region
    region[...] = jnp.zeros_like(region)
    region[:, 0:4, 0:12] = v.region_one[...].astype(jnp.float32)
    region[0:6, 0:4, 16:22] = v.region_two[...].astype(jnp.float32)
    packed = dot(bf(region[...].reshape(96, 128)), v.repeat[...]) * v.level_lanes[...]
    ids[0] = bf(dot(v.gather[...], bf(packed)))
    id_copies = [
        start(ids.at[0], ids.at[1], at(1, 0)),
        start(ids.at[0], ids.at[2], at(0, 1)),
        start(ids.at[0], ids.at[3], at(1, 1)),
        start(ids.at[0], ids.at[4], at(0, 2)),
        start(ids.at[0], ids.at[5], at(1, 2)),
    ]
    def pack_table(table, which, heads, packed):
        packed[...] = jnp.zeros_like(packed)
        for n, lane in enumerate(LATER):
            wide = min(512, PAIRS - lane)
            packed[n, :, :, 0:wide] = table[which, pl.ds(heads * odd, heads), :, lane : lane + wide]

    def unpack_table(flat, tables, heads):
        for half in range(2):
            for n, lane in enumerate(LATER):
                for h in range(heads):
                    row = 2 * (half * heads + h)
                    flat[0, row : row + 2, lane : lane + 512] = tables[half, n, h].astype(jnp.float32)

    def to_other_core(tables):
        return start(tables.at[odd], tables.at[odd], at(0, 1 - 2 * odd))

    pack_table(v.table_one, 1, H1 // 2, g.table_out_one)
    table_copy_one = start(g.table_out_one, g.table_in_one.at[odd], at(1, 0))
    pack_level(1)
    first.append(send_level(1))
    pack_table(v.table_two, 0, H2 // 2, g.table_out_two)
    table_copy_two = start(g.table_out_two, g.table_in_two.at[odd], at(1, 0))

    lane_one = lax.broadcasted_iota(jnp.int32, (D1, 256), 1)
    weight = v.project_one[...].astype(jnp.float32)
    weight_k, weight_q = g.weight_k, g.weight_q
    columns = pltpu.roll(weight[:, 128:512], 384 - 64, 1)[:, 0:256]
    weight_k[...] = bf(jnp.where(lane_one < D1, columns, 0.0))
    weight_q[...] = bf(jnp.where(lane_one < D1, weight[:, 0:256], 0.0))
    side = lax.broadcasted_iota(jnp.int32, (D2, D2), 0) == lax.broadcasted_iota(jnp.int32, (D2, D2), 1)
    eye = bf(jnp.where(side, 1.0, 0.0))
    g.turned_v_one[...] = bf(dot_t(eye[0:D1, 0:D1], bf(weight[:, 384:576])))

    def window_rows(flat, window, first_row):
        parts = []
        for zq in range(2):
            for aq in range(first_row, first_row + 3):
                pieces = []
                for zk in range(2):
                    offset = ((zq * 2 + zk) * 6 + aq) * SPAN
                    base = offset // 128 * 128
                    piece = flat[window, :, base : base + 384]
                    if offset != base:
                        piece = pltpu.roll(piece, 384 - (offset - base), 1)
                    pieces.append(piece[:, 0:256])
                parts.append(jnp.concatenate(pieces, 1))
        return bf(jnp.concatenate(parts, 0))

    def shifted(left, block, part):
        rows = part.shape[0]
        for n in range(6):
            moved = pltpu.roll(part, 512 - n, 1) if n else part
            left[block, n * rows : n * rows + rows, :] = moved

    flat_one, flat_two = g.flat_one, g.flat_two
    left_one, left_two, bias_one, bias_two = g.left_one, g.left_two, g.bias_one, g.bias_two
    flat_one[...] = jnp.zeros_like(flat_one)
    flat_two[...] = jnp.zeros_like(flat_two)

    def fill_one(ag):
        window, first_row = ((0, 3), (1, 0), (1, 3), (2, 0))[ag]
        part = dot(v.choose_one[...], window_rows(flat_one, window, first_row))
        for level in range(2):
            block = level * 4 + ag
            shifted(left_one, block, part[level * 36 : level * 36 + 36])
            left = bf(left_one[block])
            for og in range(2):
                bias_one[block, og] = dot_t(v.shift[1 - og], left)

    def fill_two(ag):
        part = dot(v.choose_two[...], window_rows(flat_two, ag, 3 - 3 * ag))
        for level in range(2):
            block = level * 2 + ag
            shifted(left_two, block, part[level * 72 : level * 72 + 72])
            bias_two[block] = dot_t(v.shift[half_own], bf(left_two[block]))

    for h in range(H1):
        for window in (1, 2):
            flat_one[window, 2 * h : 2 * h + 2, 0:PAIRS] = v.table_one[window - 1, h].astype(jnp.float32)
    for ag in (1, 2, 3):
        fill_one(ag)
    for h in range(H2):
        flat_two[1, 2 * h : 2 * h + 2, 0:PAIRS] = v.table_two[0, h].astype(jnp.float32)
    fill_two(1)
    table_copy_one.wait_recv()
    table_copy_one = to_other_core(g.table_in_one)

    for copy in id_copies:
        copy.wait_recv()
    table = v.table
    valid = g.valid[...]
    rows_global = valid.shape[1]
    lane_valid = lax.broadcasted_iota(jnp.int32, (COLUMN, rows_global), 1)
    lane_number = lax.broadcasted_iota(jnp.int32, (COLUMN, 128), 1).astype(jnp.float32)
    row_here = table[10, :, 0:rows_global].astype(jnp.int32)

    def wrap(row, extent):
        return jnp.where(row >= extent, row - extent, row)

    row = wrap(lax.rem(12 * lat + rows_global - 3, rows_global) + row_here, rows_global)
    alive = jnp.sum(jnp.where((lane_valid == row) & (valid == 1), 1.0, 0.0), -1, keepdims=True)
    row = wrap(lax.rem(6 * lat + rows_global // 2 - 3, rows_global // 2) + row_here, rows_global // 2)
    alive_two = jnp.max(jnp.where((lane_valid >> 1 == row) & (valid == 1), 1.0, 0.0), -1, keepdims=True)
    for side in range(2):
        mine = jnp.concatenate([ids[3 - 2 * side], ids[2 - 2 * side]], 0)
        picked = dot(v.rows_one[...], mine)
        for level in range(2):
            for oh in range(2):
                c = 2 * side + oh
                number = jnp.sum(picked * table[2 * level + oh], -1, keepdims=True)
                same = jnp.where(number + FEATURE == lane_number, 1.0, 0.0)
                g.key_mask[level, c] = same + (1.0 - alive) * table[6 + oh]
                if c in (1, 2):
                    g.query_mask[level, c - 1] = (table[8 + oh] - same) * (-FAR)
    for oh in range(2):
        slot = 2 * half_own + 2 - 2 * oh
        mine = jnp.concatenate([ids[slot + 1], ids[slot]], 0)
        picked = dot(v.rows_two[...], mine)
        for level in range(2):
            number = jnp.sum(picked * table[4 + level], -1, keepdims=True)
            same = jnp.where(number + FEATURE == lane_number, 1.0, 0.0)
            g.key_mask_two[level, oh] = same + (1.0 - alive_two) * table[6 + oh]
            g.query_mask_two[level, oh] = (table[8 + oh] - same) * (-FAR)

    table_copy_one.wait_recv()
    unpack_table(flat_one, g.table_in_one, H1 // 2)
    fill_one(0)

    queries, heads = g.queries, g.heads

    def section_one(level):
        for c in range(4):
            normed = normalize(ext[level, c], g.gain_one[...])
            g.normed_one[c] = normed.astype(jnp.float32)
            if c in (1, 2):
                q = dot(normed, weight_q[...]) * HEAD ** (-0.5)
                queries[c - 1, :, 0:128] = q[:, 0:128]
                queries[c - 1, :, 128:256] = q[:, 128:256] + g.query_mask[level, c - 1]
        places, tasks = [], []
        for side in range(2):
            for window in range(3):
                lo = window * 72
                pair = [g.normed_one[2 * side + oh, lo : lo + 72, :] for oh in range(2)]
                mask = [g.key_mask[level, 2 * side + oh, lo : lo + 72, :] for oh in range(2)]
                tokens = bf(jnp.concatenate(pair, 0))
                key = dot(tokens, weight_k[...])
                key = bf(jnp.concatenate([key[:, 0:128], key[:, 128:256] + jnp.concatenate(mask, 0)], 1))
                value = bf(dot_t(g.turned_v_one[...], tokens))
                for ah in ((1,), (0, 1), (0,))[window]:
                    ag = 2 * window + ah - 1
                    q = queries[side, (ag + 1) * LIVE : (ag + 1) * LIVE + HELD, :]
                    tasks.append((q, key, bias_one[level * 4 + ag, side], value))
                    places.append(side * 144 + ag * LIVE)
        parts = []
        for n in range(0, 8, TOGETHER):
            parts += attend(
                tasks[n : n + TOGETHER], v.spread_one[...], v.heads_one[...], v.turned_one[...], v.back_one[...]
            )
        for place, part in zip(places, parts):
            heads[place : place + LIVE] = part
        attended = bf(dot(bf(heads[...]), v.output_one[...]))
        own = jnp.concatenate([ext[level, 1 + og, LIVE : 5 * LIVE, :] for og in range(2)], 0)
        state = bf(own + attended.astype(jnp.float32))
        normed = normalize(state, g.gain_two[...])
        inner = dot(normed, v.up[...])
        inner = bf(0.5 * inner * (1.0 + lax.erf(inner * 0.5**0.5)))
        block = bf(state.astype(jnp.float32) + dot_t(inner, v.down[...]))
        parts = dot(v.merge[...], block)
        parts = [parts[n * 72 : n * 72 + 72] for n in range(4)]
        center = sum(jnp.sum(p, -1, keepdims=True) for p in parts) / (4 * D1)
        parts = [p - center for p in parts]
        scale = lax.rsqrt(sum(jnp.sum(p * p, -1, keepdims=True) for p in parts) / (4 * D1) + 1e-5)
        gain = g.gain_three[...].reshape(1, 4 * D1)
        coarse = sum(
            dot(bf(parts[n] * scale * gain[:, n * D1 : n * D1 + D1]), v.merge_weight[n * D1 : n * D1 + D1])
            for n in range(4)
        )
        coarse = bf(coarse).astype(jnp.float32)
        g.ext_two[level, half_own, LIVE : 3 * LIVE, :] = coarse
        g.coarse[level] = coarse
        zero = jnp.zeros((8, D2), jnp.float32)
        g.send_all[level] = bf(jnp.concatenate([coarse, zero], 0))
        g.send_end[level, 0] = bf(jnp.concatenate([coarse[0:40], zero], 0))
        g.send_end[level, 1] = bf(jnp.concatenate([coarse[32:72], zero], 0))
        to = 2 * odd - 1
        ends, into = g.send_end, g.recv_end
        return [
            start(ends.at[level, 0], into.at[level, 0, 1], at(-1, 0)),
            start(ends.at[level, 1], into.at[level, 0, 0], at(1, 0)),
            start(ends.at[level, 0], into.at[level, 1, 1], at(-1, to)),
            start(ends.at[level, 1], into.at[level, 1, 0], at(1, to)),
            start(g.send_all.at[level], g.recv_all.at[level], at(0, to)),
        ]

    def own_queries(level):
        q = dot(normalize(g.coarse[level], g.gain_four[...].reshape(1, D2)), v.project_two[:, 0:D2]) * HEAD ** (-0.5)
        g.queries_two[level, 0:72, 0:D2] = q
        g.queries_two[level, 0:72, D2:512] = g.query_mask_two[level, half_own, LIVE : 3 * LIVE, :]
        g.queries_two[level, 72:96, :] = jnp.zeros((24, 512), jnp.float32)

    heads_two, ext_two = g.heads_two_out, g.ext_two
    g.turned_v_two[...] = bf(dot_t(eye, v.project_two[:, 2 * D2 :]))

    def section_two(level):
        ext_two[level, odd, LIVE : 3 * LIVE, :] = g.recv_all[level].astype(jnp.float32)[0:72]
        for who, oh in ((0, half_own), (1, odd)):
            ext_two[level, oh, 0:LIVE, :] = g.recv_end[level, who, 0].astype(jnp.float32)[4:40]
            ext_two[level, oh, 3 * LIVE : 4 * LIVE, :] = g.recv_end[level, who, 1].astype(jnp.float32)[0:LIVE]
        for oh in range(2):
            g.normed_two[oh] = normalize(ext_two[level, oh], g.gain_four[...].reshape(1, D2)).astype(jnp.float32)
        tasks = []
        for ag in range(2):
            lo = ag * 72
            tokens = bf(jnp.concatenate([g.normed_two[oh, lo : lo + 72, :] for oh in range(2)], 0))
            mask = jnp.concatenate([g.key_mask_two[level, oh, lo : lo + 72, :] for oh in range(2)], 0)
            tasks.append(
                (
                    g.queries_two[level, ag * LIVE : ag * LIVE + HELD, :],
                    bf(jnp.concatenate([dot(tokens, v.project_two[:, D2 : 2 * D2]), mask], 1)),
                    bias_two[level * 2 + ag],
                    bf(dot_t(g.turned_v_two[...], tokens)),
                )
            )
        parts = attend(tasks, v.spread_two[...], v.heads_two[...], v.turned_two[...], v.back_two[...])
        for ag in range(2):
            heads_two[level, ag * LIVE : ag * LIVE + LIVE] = parts[ag]
        attended = bf(dot(bf(heads_two[level]), v.output_two[...]))
        return g.coarse[level] + attended.astype(jnp.float32)

    def wait_all(group):
        for copy in group:
            copy.wait_recv()

    wait_all(first[0])
    unpack_level(0)
    second = [section_one(0)]
    own_queries(0)
    wait_all(first[1])
    table_copy_two.wait_recv()
    table_copy_two = to_other_core(g.table_in_two)
    unpack_level(1)
    second.append(section_one(1))
    own_queries(1)

    table_copy_two.wait_recv()
    unpack_table(flat_two, g.table_in_two, H2 // 2)
    fill_two(0)

    wait_all(second[0])
    refined = [section_two(0)]
    wait_all(second[1])
    refined.append(section_two(1))
    placed = dot(v.final[...], bf(jnp.concatenate(refined, 0))).reshape(36, 8, D2)
    for i in range(6):
        g.out[i] = bf(placed[6 * i : 6 * i + 6, 0:4])
    for copy in copies:
        copy.wait_send()


def shards(
    lat_size,
    lon_size,
    fields,
    region_one,
    region_two,
    valid_rows,
    gain_one,
    project_one,
    output_one,
    table_one,
    gain_two,
    up,
    down,
    gain_three,
    merge_weight,
    gain_four,
    project_two,
    output_two,
    table_two,
):
    c = types.SimpleNamespace(**{name: jnp.asarray(value) for name, value in constants().items()})
    direct = dict(
        valid=valid_rows[None],
        gain_one=gain_one[None],
        gain_two=gain_two[None],
        gain_three=gain_three,
        gain_four=gain_four,
    )
    fetched = dict(
        fields=fields.transpose(1, 2, 0, 3),
        split=c.split,
        region_one=region_one.transpose(1, 0, 2),
        region_two=region_two.transpose(1, 0, 2),
        repeat=c.repeat,
        level_lanes=c.level_lanes,
        gather=c.gather,
        table_one=table_one.transpose(0, 2, 1, 3),
        choose_one=c.choose_one,
        shift=c.shift,
        project_one=project_one,
        rows_one=c.rows_one,
        table=c.table,
        table_two=table_two.transpose(0, 2, 1, 3),
        choose_two=c.choose_two,
        rows_two=c.rows_two,
        spread_one=c.spread_one,
        heads_one=c.heads_one,
        turned_one=c.turned_one,
        back_one=c.back_one,
        output_one=output_one,
        up=up,
        down=down.T,
        merge=c.merge,
        merge_weight=merge_weight,
        project_two=project_two,
        spread_two=c.spread_two,
        heads_two=c.heads_two,
        turned_two=c.turned_two,
        back_two=c.back_two,
        output_two=output_two,
        final=c.final,
    )
    operands = direct | fetched
    names = tuple(operands)
    f32, b16 = jnp.float32, jnp.bfloat16
    vmem = pltpu.VMEM
    scratch = dict(
        ext=vmem((2, 4, COLUMN, D1), f32),
        rows_in=vmem((12, 12, 8, D1), f32),
        send_lon=vmem((2, 2, 224, 128), b16),
        recv_lon=vmem((2, 2, 224, 128), b16),
        stage=vmem((112, 128), f32),
        send_lat=vmem((2, 2, 112, 128), b16),
        recv_lat=vmem((2, 2, 112, 128), b16),
        send_corner=vmem((2, 4, 64, 128), b16),
        recv_corner=vmem((2, 4, 64, 128), b16),
        send_all=vmem((2, 80, D2), b16),
        recv_all=vmem((2, 80, D2), b16),
        send_end=vmem((2, 2, 48, D2), b16),
        recv_end=vmem((2, 2, 2, 48, D2), b16),
        ids=vmem((6, 16, 128), b16),
        region=vmem((12, 8, 128), f32),
        table_out_one=vmem((4, H1 // 2, 2, 512), b16),
        table_out_two=vmem((4, H2 // 2, 2, 512), b16),
        table_in_one=vmem((2, 4, H1 // 2, 2, 512), b16),
        table_in_two=vmem((2, 4, H2 // 2, 2, 512), b16),
        flat_one=vmem((3, 16, TABLE), f32),
        flat_two=vmem((2, 24, TABLE), f32),
        left_one=vmem((8, 216, 512), f32),
        left_two=vmem((4, 432, 512), f32),
        bias_one=vmem((8, 2, KEYS, 216), f32),
        bias_two=vmem((4, KEYS, 432), f32),
        weight_k=vmem((D1, 256), b16),
        turned_v_one=vmem((D1, D1), b16),
        turned_v_two=vmem((D2, D2), b16),
        weight_q=vmem((D1, 256), b16),
        key_mask=vmem((2, 4, COLUMN, 128), f32),
        query_mask=vmem((2, 2, COLUMN, 128), f32),
        key_mask_two=vmem((2, 2, COLUMN, 128), f32),
        query_mask_two=vmem((2, 2, COLUMN, 128), f32),
        normed_one=vmem((4, COLUMN, D1), f32),
        queries=vmem((2, COLUMN, 256), f32),
        heads=vmem((288, D1), f32),
        ext_two=vmem((2, 2, 144, D2), f32),
        coarse=vmem((2, 72, D2), f32),
        normed_two=vmem((2, 144, D2), f32),
        queries_two=vmem((2, 96, 512), f32),
        heads_two_out=vmem((2, 72, D2), f32),
    )
    held = [vmem(x.shape, x.dtype) for x in fetched.values()]
    sems = dict(
        send=pltpu.SemaphoreType.DMA((35,)),
        recv=pltpu.SemaphoreType.DMA((35,)),
        load=pltpu.SemaphoreType.DMA((len(fetched),)),
    )
    spec = lambda name: pl.BlockSpec(memory_space=pl.ANY if name in fetched else vmem)
    scratch |= sems
    out = pl.pallas_call(
        functools.partial(kernel, lat_size, lon_size, names, tuple(fetched), tuple(scratch)),
        out_shape=jax.ShapeDtypeStruct((6, 6, 4, D2), b16),
        in_specs=[spec(name) for name in names],
        out_specs=pl.BlockSpec(memory_space=vmem),
        scratch_shapes=held + list(scratch.values()),
        compiler_params=pltpu.CompilerParams(
            collective_id=0, has_side_effects=True, vmem_limit_bytes=60 * 1024 * 1024
        ),
        name="block",
    )(*operands.values())
    return out.transpose(2, 0, 1, 3)


def solution(mesh):
    split = P(None, "lat", "lon")
    table = P("lat", None, None, None)
    placed = (P(None, "lat", "lon", None), split, split) + (P(),) * 4 + (table,) + (P(),) * 8 + (table,)
    return jax.shard_map(
        functools.partial(shards, mesh.shape["lat"], mesh.shape["lon"]),
        mesh=mesh,
        in_specs=placed,
        out_specs=P(None, "lat", "lon", None),
        check_vma=False,
    )
```

```python
import functools
import types

import jax
import jax.numpy as jnp
import ml_dtypes
import numpy as np
from jax import lax
from jax.experimental import pallas as pl
from jax.experimental.pallas import tpu as pltpu
from jax.sharding import PartitionSpec as P

D1, H1, MLP = 192, 6, 768
D2, H2 = 384, 12
HEAD = 32
LIVE = 36
HELD = 48
KEYS = 4 * LIVE
COLUMN = 6 * LIVE
PAIRS = 3312
SPAN = 6 * 23
TABLE = 3456
LATER = (384, 1152, 2048, 2816)
FAR = 2.0**100
MESH = pl.DeviceIdType.MESH
LEVELS = ((1, 2), (3, 0))
TOGETHER = 8
FEATURE = 64


def atom_rows():
    return [((z * 3 + a) * 6 + o, z, a, o) for z in range(2) for a in range(3) for o in range(6)]


@functools.lru_cache(None)
def constants():
    split = np.zeros((2, 2, 40, 3, 12, 8), np.float32)
    for level in range(2):
        for og in range(2):
            for r, z, a, o in atom_rows():
                split[level, og, r, a, og * 6 + o, LEVELS[level][z]] = 1

    def spread(heads):
        rows = np.zeros((6, heads, 6, HELD), np.float32)
        for r, z, a, o in atom_rows():
            rows[o, :, z * 3 + a, r] = 1
        return rows.reshape(-1, HELD)

    def head_mask(heads, lanes):
        mask = np.zeros((6, heads, 6, lanes), np.float32)
        for h in range(heads):
            mask[:, h, :, h * HEAD : (h + 1) * HEAD] = 1
        mask[..., heads * HEAD :] = 1
        return mask.reshape(-1, lanes)

    def choose(heads, padded):
        sel = np.zeros((2, heads, 6, 6, padded), np.float32)
        for level in range(2):
            for h in range(heads):
                for za in range(6):
                    sel[level, h, za, za, 2 * h + level] = 1
        return sel.reshape(2 * heads * 6, 6 * padded)

    shift = np.zeros((2, KEYS, 512), np.float32)
    for half in range(2):
        for ah in range(2):
            for oh in range(2):
                for r, z, a, o in atom_rows():
                    lane = z * 256 + (3 * ah + a) * 23 + 6 * half - (6 * oh + o) + 11
                    shift[half, (oh * 2 + ah) * LIVE + r, lane] = 1

    repeat = np.zeros((128, 128), np.float32)
    level_lanes = np.zeros((12, 8, 128), np.float32)
    gather = np.zeros((16, 12, 8), np.float32)
    for z in range(4):
        for n in range(32):
            repeat[n, z * 32 + n] = 1
        level_lanes[:, z, z * 32 : z * 32 + 32] = 1
        for a in range(12):
            gather[a, a, z] = 1
    rows_one = np.zeros((COLUMN, 32), np.float32)
    rows_two = np.zeros((COLUMN, 32), np.float32)
    table = np.zeros((11, COLUMN, 128), np.float32)
    table[8:10, :, FEATURE : FEATURE + 4] = 1
    table[8:10, :, FEATURE + 5 : FEATURE + 25] = 1
    for ag in range(6):
        for r, z, a, o in atom_rows():
            k = ag * LIVE + r
            window, ah = ag // 2, ag % 2
            rows_one[k, (0 if window == 0 else 16) + (6, 0, 6)[window] + 3 * ah + a] = 1
            if ag < 4:
                rows_two[k, 16 * window + 3 * ah + a] = 1
            table[10, k, :] = 3 * ag + a
            for level in range(2):
                table[4 + level, k, (2 * level + z) * 32 + 16 + o] = 1
                for oh in range(2):
                    table[2 * level + oh, k, (2 * level + z) * 32 + 6 * oh + o] = 1
            for oh in range(2):
                for at in (5 + z, 7 + 3 * ah + a, 13 + 6 * oh + o):
                    table[6 + oh, k, FEATURE + at] = 1
                    table[8 + oh, k, FEATURE + at] = 0

    merge = np.zeros((4, 2, LIVE, 2, 4, LIVE), np.float32)
    for da in range(2):
        for do in range(2):
            for half in range(2):
                for r, z, a, o in atom_rows():
                    row, col = 2 * (3 * half + a) + da, 2 * o + do
                    at = (z * 3 + row % 3) * 6 + col % 6
                    merge[da * 2 + do, half, r, col // 6, row // 3, at] = 1
    final = np.zeros((6, 6, 8, 2, 2, LIVE), np.float32)
    for level in range(2):
        for half in range(2):
            for r, z, a, o in atom_rows():
                final[3 * half + a, o, LEVELS[level][z], level, half, r] = 1
    b = lambda x: x.astype(ml_dtypes.bfloat16)
    flip = lambda x: np.concatenate([x.T[:LIVE], np.zeros((4, x.shape[0]), np.float32)])
    return dict(
        split=b(split.reshape(160, 288)),
        repeat=b(repeat),
        level_lanes=level_lanes.reshape(96, 128),
        gather=b(gather.reshape(16, 96)),
        choose_one=b(choose(H1, 16)),
        choose_two=b(choose(H2, 24)),
        shift=b(shift),
        rows_one=b(rows_one),
        rows_two=b(rows_two),
        table=table,
        spread_one=b(spread(H1)),
        heads_one=b(head_mask(H1, 256)),
        turned_one=b(head_mask(H1, D1).T),
        back_one=b(flip(spread(H1))),
        merge=b(merge.reshape(288, 288)),
        spread_two=b(spread(H2)),
        heads_two=b(head_mask(H2, 512)),
        turned_two=b(head_mask(H2, D2).T),
        back_two=b(flip(spread(H2))),
        final=b(final.reshape(288, 144)),
    )


def dot(a, b):
    return jnp.dot(a, b, preferred_element_type=jnp.float32)


def dot_t(a, b):
    return lax.dot_general(a, b, (((1,), (1,)), ((), ())), preferred_element_type=jnp.float32)


def bf(x):
    return x.astype(jnp.bfloat16)


def normalize(x, gain):
    x = x.astype(jnp.float32)
    x = x - jnp.mean(x, -1, keepdims=True)
    var = jnp.mean(x * x, -1, keepdims=True)
    return bf(x * lax.rsqrt(var + 1e-5) * gain)


def attend(tasks, spread, head_mask, turned_mask, back):
    qs = [bf(dot(spread, bf(q))) * head_mask for q, _, _, _ in tasks]
    scores = [dot_t(key, q) + bias for q, (_, key, bias, _) in zip(qs, tasks)]
    weights = [jnp.exp(s - jnp.max(s, 0, keepdims=True)) for s in scores]
    probs = [bf(w * (1.0 / jnp.sum(w, 0, keepdims=True))) for w in weights]
    mixed = [bf(dot(value, p)) * turned_mask for p, (_, _, _, value) in zip(probs, tasks)]
    return [dot_t(back, m)[0:LIVE] for m in mixed]


def kernel(lat_size, lon_size, names, fetched, scratch_names, *refs):
    g = types.SimpleNamespace(**dict(zip(names, refs[: len(names)], strict=True)))
    refs = refs[len(names) :]
    g.out = refs[0]
    g.held = dict(zip(fetched, refs[1 : 1 + len(fetched)], strict=True))
    for name, ref in zip(scratch_names, refs[1 + len(fetched) :], strict=True):
        setattr(g, name, ref)
    send, recv, load = g.send, g.recv, g.load
    lat, lon = lax.axis_index("lat"), lax.axis_index("lon")
    odd = lax.rem(lon, 2)
    half_own = 1 - odd

    def at(dlat, dlon):
        return (lax.rem(lat + dlat + lat_size, lat_size), lax.rem(lon + dlon + lon_size, lon_size))

    around = [(a, o) for a in (-1, 0, 1) for o in (-1, 0, 1) if (a, o) != (0, 0)]
    barrier = pltpu.get_barrier_semaphore()
    for a, o in around + [(0, -2), (-1, -2)]:
        pl.semaphore_signal(barrier, inc=1, device_id=at(a, o), device_id_type=MESH)

    class Held:
        def __init__(self):
            self.loads = {}
            for n, name in enumerate(fetched):
                self.loads[name] = pltpu.make_async_copy(getattr(g, name), g.held[name], load.at[n])
                self.loads[name].start()

        def __getattr__(self, name):
            self.loads[name].wait()
            ref = g.held[name]
            setattr(self, name, ref)
            return ref

    v = Held()
    copies = []

    def start(src, dst, target):
        n = len(copies)
        copy = pltpu.make_async_remote_copy(
            src_ref=src, dst_ref=dst, send_sem=send.at[n], recv_sem=recv.at[n], device_id=target, device_id_type=MESH
        )
        copies.append(copy)
        copy.start()
        return copy

    ext, rows_in = g.ext, g.rows_in
    rows_in[...] = jnp.zeros_like(rows_in)
    for a in range(12):
        rows_in[a, :, 0:4, :] = v.fields[a].astype(jnp.float32)
    for ag in range(4):
        moved = dot(v.split[...], bf(rows_in[3 * ag : 3 * ag + 3].reshape(288, D1)))
        for level in range(2):
            for og in range(2):
                lo = (level * 2 + og) * 40
                ext[level, 1 + og, (1 + ag) * LIVE : (2 + ag) * LIVE, :] = moved[lo : lo + LIVE]

    g.stage[...] = jnp.zeros_like(g.stage)

    def pack_level(level):
        for og in range(2):
            x = ext[level, 1 + og, LIVE : 5 * LIVE, :]
            tail = jnp.concatenate([x[0:72, 128:192], x[72:144, 128:192]], 1)
            tail = jnp.concatenate([tail, jnp.zeros((8, 128), jnp.float32)], 0)
            g.send_lon[level, og] = bf(jnp.concatenate([x[:, 0:128], tail], 0))
        for end in range(2):
            lo = (1 + 3 * end) * LIVE
            stage = g.stage
            for og in range(2):
                stage[og * LIVE : og * LIVE + LIVE, :] = ext[level, 1 + og, lo : lo + LIVE, 0:128]
            tail = [ext[level, 1 + og, lo : lo + LIVE, 128:192] for og in range(2)]
            stage[72:108, :] = jnp.concatenate(tail, 1)
            g.send_lat[level, end] = bf(stage[...])
            for og in range(2):
                main = ext[level, 1 + og, lo : lo + 40, 0:128]
                tail = [ext[level, 1 + og, lo + n : lo + n + 24, 128:192] for n in (0, 18)]
                g.send_corner[level, 2 * end + og] = bf(jnp.concatenate([main, jnp.concatenate(tail, 1)], 0))

    def send_level(level):
        lon_s, lat_s, cor_s = g.send_lon, g.send_lat, g.send_corner
        lon_r, lat_r, cor_r = g.recv_lon, g.recv_lat, g.recv_corner
        return [
            start(lon_s.at[level, 0], lon_r.at[level, 1], at(0, -1)),
            start(lon_s.at[level, 1], lon_r.at[level, 0], at(0, 1)),
            start(lat_s.at[level, 0], lat_r.at[level, 1], at(-1, 0)),
            start(lat_s.at[level, 1], lat_r.at[level, 0], at(1, 0)),
            start(cor_s.at[level, 0], cor_r.at[level, 3], at(-1, -1)),
            start(cor_s.at[level, 1], cor_r.at[level, 2], at(-1, 1)),
            start(cor_s.at[level, 2], cor_r.at[level, 1], at(1, -1)),
            start(cor_s.at[level, 3], cor_r.at[level, 0], at(1, 1)),
        ]

    def unpack_level(level):
        for side in range(2):
            x = g.recv_lon[level, side].astype(jnp.float32)
            c = 3 * side
            ext[level, c, LIVE : 5 * LIVE, 0:128] = x[0:144]
            ext[level, c, LIVE : 3 * LIVE, 128:192] = x[144:216, 0:64]
            ext[level, c, 3 * LIVE : 5 * LIVE, 128:192] = x[144:216, 64:128]
            for end in range(2):
                y = g.recv_corner[level, 2 * end + side].astype(jnp.float32)
                lo = 5 * LIVE * end
                ext[level, c, lo : lo + LIVE, 0:128] = y[0:LIVE]
                for n in range(2):
                    ext[level, c, lo + 18 * n : lo + 18 * n + 18, 128:192] = y[40:58, 64 * n : 64 * n + 64]
        for end in range(2):
            x = g.recv_lat[level, end].astype(jnp.float32)
            lo = 5 * LIVE * end
            for og in range(2):
                ext[level, 1 + og, lo : lo + LIVE, 0:128] = x[og * LIVE : og * LIVE + LIVE]
                ext[level, 1 + og, lo : lo + LIVE, 128:192] = x[72:108, og * 64 : og * 64 + 64]

    pack_level(0)
    pl.semaphore_wait(barrier, 10)
    first = [send_level(0)]

    ids, region = g.ids, g.region
    region[...] = jnp.zeros_like(region)
    region[:, 0:4, 0:12] = v.region_one[...].astype(jnp.float32)
    region[0:6, 0:4, 16:22] = v.region_two[...].astype(jnp.float32)
    packed = dot(bf(region[...].reshape(96, 128)), v.repeat[...]) * v.level_lanes[...]
    ids[0] = bf(dot(v.gather[...], bf(packed)))
    id_copies = [
        start(ids.at[0], ids.at[1], at(1, 0)),
        start(ids.at[0], ids.at[2], at(0, 1)),
        start(ids.at[0], ids.at[3], at(1, 1)),
        start(ids.at[0], ids.at[4], at(0, 2)),
        start(ids.at[0], ids.at[5], at(1, 2)),
    ]
    def pack_table(table, which, heads, packed):
        packed[...] = jnp.zeros_like(packed)
        for n, lane in enumerate(LATER):
            wide = min(512, PAIRS - lane)
            packed[n, :, :, 0:wide] = table[which, pl.ds(heads * odd, heads), :, lane : lane + wide]

    def unpack_table(flat, tables, heads):
        for half in range(2):
            for n, lane in enumerate(LATER):
                for h in range(heads):
                    row = 2 * (half * heads + h)
                    flat[0, row : row + 2, lane : lane + 512] = tables[half, n, h].astype(jnp.float32)

    def to_other_core(tables):
        return start(tables.at[odd], tables.at[odd], at(0, 1 - 2 * odd))

    pack_table(v.table_one, 1, H1 // 2, g.table_out_one)
    table_copy_one = start(g.table_out_one, g.table_in_one.at[odd], at(1, 0))
    pack_level(1)
    first.append(send_level(1))
    pack_table(v.table_two, 0, H2 // 2, g.table_out_two)
    table_copy_two = start(g.table_out_two, g.table_in_two.at[odd], at(1, 0))

    lane_one = lax.broadcasted_iota(jnp.int32, (D1, 256), 1)
    weight = v.project_one[...].astype(jnp.float32)
    weight_k, weight_q = g.weight_k, g.weight_q
    columns = pltpu.roll(weight[:, 128:512], 384 - 64, 1)[:, 0:256]
    weight_k[...] = bf(jnp.where(lane_one < D1, columns, 0.0))
    weight_q[...] = bf(jnp.where(lane_one < D1, weight[:, 0:256], 0.0))
    side = lax.broadcasted_iota(jnp.int32, (D2, D2), 0) == lax.broadcasted_iota(jnp.int32, (D2, D2), 1)
    eye = bf(jnp.where(side, 1.0, 0.0))
    g.turned_v_one[...] = bf(dot_t(eye[0:D1, 0:D1], bf(weight[:, 384:576])))

    def window_rows(flat, window, first_row):
        parts = []
        for zq in range(2):
            for aq in range(first_row, first_row + 3):
                pieces = []
                for zk in range(2):
                    offset = ((zq * 2 + zk) * 6 + aq) * SPAN
                    base = offset // 128 * 128
                    piece = flat[window, :, base : base + 384]
                    if offset != base:
                        piece = pltpu.roll(piece, 384 - (offset - base), 1)
                    pieces.append(piece[:, 0:256])
                parts.append(jnp.concatenate(pieces, 1))
        return bf(jnp.concatenate(parts, 0))

    def shifted(left, block, part):
        rows = part.shape[0]
        for n in range(6):
            moved = pltpu.roll(part, 512 - n, 1) if n else part
            left[block, n * rows : n * rows + rows, :] = moved

    flat_one, flat_two = g.flat_one, g.flat_two
    left_one, left_two, bias_one, bias_two = g.left_one, g.left_two, g.bias_one, g.bias_two
    flat_one[...] = jnp.zeros_like(flat_one)
    flat_two[...] = jnp.zeros_like(flat_two)

    def expand_one(block):
        left = bf(left_one[block])
        for og in range(2):
            bias_one[block, og] = dot_t(v.shift[1 - og], left)

    def fill_one(ag):
        window, first_row = ((0, 3), (1, 0), (1, 3), (2, 0))[ag]
        part = dot(v.choose_one[...], window_rows(flat_one, window, first_row))
        for level in range(2):
            block = level * 4 + ag
            shifted(left_one, block, part[level * 36 : level * 36 + 36])
            if level == 0:
                expand_one(block)

    def fill_two(ag):
        part = dot(v.choose_two[...], window_rows(flat_two, ag, 3 - 3 * ag))
        for level in range(2):
            block = level * 2 + ag
            shifted(left_two, block, part[level * 72 : level * 72 + 72])
            bias_two[block] = dot_t(v.shift[half_own], bf(left_two[block]))

    for h in range(H1):
        for window in (1, 2):
            flat_one[window, 2 * h : 2 * h + 2, 0:PAIRS] = v.table_one[window - 1, h].astype(jnp.float32)
    for ag in (1, 2, 3):
        fill_one(ag)
    for h in range(H2):
        flat_two[1, 2 * h : 2 * h + 2, 0:PAIRS] = v.table_two[0, h].astype(jnp.float32)
    fill_two(1)
    table_copy_one.wait_recv()
    table_copy_one = to_other_core(g.table_in_one)

    for copy in id_copies:
        copy.wait_recv()
    table = v.table
    valid = g.valid[...]
    rows_global = valid.shape[1]
    lane_valid = lax.broadcasted_iota(jnp.int32, (COLUMN, rows_global), 1)
    lane_number = lax.broadcasted_iota(jnp.int32, (COLUMN, 128), 1).astype(jnp.float32)
    row_here = table[10, :, 0:rows_global].astype(jnp.int32)

    def wrap(row, extent):
        return jnp.where(row >= extent, row - extent, row)

    row = wrap(lax.rem(12 * lat + rows_global - 3, rows_global) + row_here, rows_global)
    alive = jnp.sum(jnp.where((lane_valid == row) & (valid == 1), 1.0, 0.0), -1, keepdims=True)
    row = wrap(lax.rem(6 * lat + rows_global // 2 - 3, rows_global // 2) + row_here, rows_global // 2)
    alive_two = jnp.max(jnp.where((lane_valid >> 1 == row) & (valid == 1), 1.0, 0.0), -1, keepdims=True)
    for side in range(2):
        mine = jnp.concatenate([ids[3 - 2 * side], ids[2 - 2 * side]], 0)
        picked = dot(v.rows_one[...], mine)
        for level in range(2):
            for oh in range(2):
                c = 2 * side + oh
                number = jnp.sum(picked * table[2 * level + oh], -1, keepdims=True)
                same = jnp.where(number + FEATURE == lane_number, 1.0, 0.0)
                g.key_mask[level, c] = same + (1.0 - alive) * table[6 + oh]
                if c in (1, 2):
                    g.query_mask[level, c - 1] = (table[8 + oh] - same) * (-FAR)
    for oh in range(2):
        slot = 2 * half_own + 2 - 2 * oh
        mine = jnp.concatenate([ids[slot + 1], ids[slot]], 0)
        picked = dot(v.rows_two[...], mine)
        for level in range(2):
            number = jnp.sum(picked * table[4 + level], -1, keepdims=True)
            same = jnp.where(number + FEATURE == lane_number, 1.0, 0.0)
            g.key_mask_two[level, oh] = same + (1.0 - alive_two) * table[6 + oh]
            g.query_mask_two[level, oh] = (table[8 + oh] - same) * (-FAR)

    table_copy_one.wait_recv()
    unpack_table(flat_one, g.table_in_one, H1 // 2)
    fill_one(0)

    queries, heads = g.queries, g.heads

    def section_one(level):
        for c in range(4):
            normed = normalize(ext[level, c], g.gain_one[...])
            g.normed_one[c] = normed.astype(jnp.float32)
            if c in (1, 2):
                q = dot(normed, weight_q[...]) * HEAD ** (-0.5)
                queries[c - 1, :, 0:128] = q[:, 0:128]
                queries[c - 1, :, 128:256] = q[:, 128:256] + g.query_mask[level, c - 1]
        places, tasks = [], []
        for side in range(2):
            for window in range(3):
                lo = window * 72
                pair = [g.normed_one[2 * side + oh, lo : lo + 72, :] for oh in range(2)]
                mask = [g.key_mask[level, 2 * side + oh, lo : lo + 72, :] for oh in range(2)]
                tokens = bf(jnp.concatenate(pair, 0))
                key = dot(tokens, weight_k[...])
                key = bf(jnp.concatenate([key[:, 0:128], key[:, 128:256] + jnp.concatenate(mask, 0)], 1))
                value = bf(dot_t(g.turned_v_one[...], tokens))
                for ah in ((1,), (0, 1), (0,))[window]:
                    ag = 2 * window + ah - 1
                    q = queries[side, (ag + 1) * LIVE : (ag + 1) * LIVE + HELD, :]
                    tasks.append((q, key, bias_one[level * 4 + ag, side], value))
                    places.append(side * 144 + ag * LIVE)
        parts = []
        for n in range(0, 8, TOGETHER):
            parts += attend(
                tasks[n : n + TOGETHER], v.spread_one[...], v.heads_one[...], v.turned_one[...], v.back_one[...]
            )
        for place, part in zip(places, parts):
            heads[place : place + LIVE] = part
        attended = bf(dot(bf(heads[...]), v.output_one[...]))
        own = jnp.concatenate([ext[level, 1 + og, LIVE : 5 * LIVE, :] for og in range(2)], 0)
        state = bf(own + attended.astype(jnp.float32))
        normed = normalize(state, g.gain_two[...])
        inner = dot(normed, v.up[...])
        inner = bf(0.5 * inner * (1.0 + lax.erf(inner * 0.5**0.5)))
        block = bf(state.astype(jnp.float32) + dot_t(inner, v.down[...]))
        parts = dot(v.merge[...], block)
        parts = [parts[n * 72 : n * 72 + 72] for n in range(4)]
        center = sum(jnp.sum(p, -1, keepdims=True) for p in parts) / (4 * D1)
        parts = [p - center for p in parts]
        scale = lax.rsqrt(sum(jnp.sum(p * p, -1, keepdims=True) for p in parts) / (4 * D1) + 1e-5)
        gain = g.gain_three[...].reshape(1, 4 * D1)
        coarse = sum(
            dot(bf(parts[n] * scale * gain[:, n * D1 : n * D1 + D1]), v.merge_weight[n * D1 : n * D1 + D1])
            for n in range(4)
        )
        coarse = bf(coarse).astype(jnp.float32)
        g.ext_two[level, half_own, LIVE : 3 * LIVE, :] = coarse
        g.coarse[level] = coarse
        zero = jnp.zeros((8, D2), jnp.float32)
        g.send_all[level] = bf(jnp.concatenate([coarse, zero], 0))
        g.send_end[level, 0] = bf(jnp.concatenate([coarse[0:40], zero], 0))
        g.send_end[level, 1] = bf(jnp.concatenate([coarse[32:72], zero], 0))
        to = 2 * odd - 1
        ends, into = g.send_end, g.recv_end
        return [
            start(g.send_all.at[level], g.recv_all.at[level], at(0, to)),
            start(ends.at[level, 0], into.at[level, 0, 1], at(-1, 0)),
            start(ends.at[level, 1], into.at[level, 0, 0], at(1, 0)),
            start(ends.at[level, 0], into.at[level, 1, 1], at(-1, to)),
            start(ends.at[level, 1], into.at[level, 1, 0], at(1, to)),
        ]

    def own_queries(level):
        q = dot(normalize(g.coarse[level], g.gain_four[...].reshape(1, D2)), v.project_two[:, 0:D2]) * HEAD ** (-0.5)
        g.queries_two[level, 0:72, 0:D2] = q
        g.queries_two[level, 0:72, D2:512] = g.query_mask_two[level, half_own, LIVE : 3 * LIVE, :]
        g.queries_two[level, 72:96, :] = jnp.zeros((24, 512), jnp.float32)

    heads_two, ext_two = g.heads_two_out, g.ext_two
    g.turned_v_two[...] = bf(dot_t(eye, v.project_two[:, 2 * D2 :]))

    def section_two(level):
        ext_two[level, odd, LIVE : 3 * LIVE, :] = g.recv_all[level].astype(jnp.float32)[0:72]
        for who, oh in ((0, half_own), (1, odd)):
            ext_two[level, oh, 0:LIVE, :] = g.recv_end[level, who, 0].astype(jnp.float32)[4:40]
            ext_two[level, oh, 3 * LIVE : 4 * LIVE, :] = g.recv_end[level, who, 1].astype(jnp.float32)[0:LIVE]
        for oh in range(2):
            g.normed_two[oh] = normalize(ext_two[level, oh], g.gain_four[...].reshape(1, D2)).astype(jnp.float32)
        tasks = []
        for ag in range(2):
            lo = ag * 72
            tokens = bf(jnp.concatenate([g.normed_two[oh, lo : lo + 72, :] for oh in range(2)], 0))
            mask = jnp.concatenate([g.key_mask_two[level, oh, lo : lo + 72, :] for oh in range(2)], 0)
            tasks.append(
                (
                    g.queries_two[level, ag * LIVE : ag * LIVE + HELD, :],
                    bf(jnp.concatenate([dot(tokens, v.project_two[:, D2 : 2 * D2]), mask], 1)),
                    bias_two[level * 2 + ag],
                    bf(dot_t(g.turned_v_two[...], tokens)),
                )
            )
        parts = attend(tasks, v.spread_two[...], v.heads_two[...], v.turned_two[...], v.back_two[...])
        for ag in range(2):
            heads_two[level, ag * LIVE : ag * LIVE + LIVE] = parts[ag]
        attended = bf(dot(bf(heads_two[level]), v.output_two[...]))
        return g.coarse[level] + attended.astype(jnp.float32)

    def wait_all(group):
        for copy in group:
            copy.wait_recv()

    wait_all(first[0])
    unpack_level(0)
    second = [section_one(0)]
    own_queries(0)
    for block in range(4, 8):
        expand_one(block)
    wait_all(first[1])
    table_copy_two.wait_recv()
    table_copy_two = to_other_core(g.table_in_two)
    unpack_level(1)
    second.append(section_one(1))
    own_queries(1)

    table_copy_two.wait_recv()
    unpack_table(flat_two, g.table_in_two, H2 // 2)
    fill_two(0)

    wait_all(second[0])
    refined = [section_two(0)]
    wait_all(second[1])
    refined.append(section_two(1))
    placed = dot(v.final[...], bf(jnp.concatenate(refined, 0))).reshape(36, 8, D2)
    for i in range(6):
        g.out[i] = bf(placed[6 * i : 6 * i + 6, 0:4])
    for copy in copies:
        copy.wait_send()


def shards(
    lat_size,
    lon_size,
    fields,
    region_one,
    region_two,
    valid_rows,
    gain_one,
    project_one,
    output_one,
    table_one,
    gain_two,
    up,
    down,
    gain_three,
    merge_weight,
    gain_four,
    project_two,
    output_two,
    table_two,
):
    c = types.SimpleNamespace(**{name: jnp.asarray(value) for name, value in constants().items()})
    direct = dict(
        valid=valid_rows[None],
        gain_one=gain_one[None],
        gain_two=gain_two[None],
        gain_three=gain_three,
        gain_four=gain_four,
    )
    fetched = dict(
        fields=fields.transpose(1, 2, 0, 3),
        split=c.split,
        region_one=region_one.transpose(1, 0, 2),
        region_two=region_two.transpose(1, 0, 2),
        repeat=c.repeat,
        level_lanes=c.level_lanes,
        gather=c.gather,
        table_one=table_one.transpose(0, 2, 1, 3),
        choose_one=c.choose_one,
        shift=c.shift,
        project_one=project_one,
        rows_one=c.rows_one,
        table=c.table,
        table_two=table_two.transpose(0, 2, 1, 3),
        choose_two=c.choose_two,
        rows_two=c.rows_two,
        spread_one=c.spread_one,
        heads_one=c.heads_one,
        turned_one=c.turned_one,
        back_one=c.back_one,
        output_one=output_one,
        up=up,
        down=down.T,
        merge=c.merge,
        merge_weight=merge_weight,
        project_two=project_two,
        spread_two=c.spread_two,
        heads_two=c.heads_two,
        turned_two=c.turned_two,
        back_two=c.back_two,
        output_two=output_two,
        final=c.final,
    )
    operands = direct | fetched
    names = tuple(operands)
    f32, b16 = jnp.float32, jnp.bfloat16
    vmem = pltpu.VMEM
    scratch = dict(
        ext=vmem((2, 4, COLUMN, D1), f32),
        rows_in=vmem((12, 12, 8, D1), f32),
        send_lon=vmem((2, 2, 224, 128), b16),
        recv_lon=vmem((2, 2, 224, 128), b16),
        stage=vmem((112, 128), f32),
        send_lat=vmem((2, 2, 112, 128), b16),
        recv_lat=vmem((2, 2, 112, 128), b16),
        send_corner=vmem((2, 4, 64, 128), b16),
        recv_corner=vmem((2, 4, 64, 128), b16),
        send_all=vmem((2, 80, D2), b16),
        recv_all=vmem((2, 80, D2), b16),
        send_end=vmem((2, 2, 48, D2), b16),
        recv_end=vmem((2, 2, 2, 48, D2), b16),
        ids=vmem((6, 16, 128), b16),
        region=vmem((12, 8, 128), f32),
        table_out_one=vmem((4, H1 // 2, 2, 512), b16),
        table_out_two=vmem((4, H2 // 2, 2, 512), b16),
        table_in_one=vmem((2, 4, H1 // 2, 2, 512), b16),
        table_in_two=vmem((2, 4, H2 // 2, 2, 512), b16),
        flat_one=vmem((3, 16, TABLE), f32),
        flat_two=vmem((2, 24, TABLE), f32),
        left_one=vmem((8, 216, 512), f32),
        left_two=vmem((4, 432, 512), f32),
        bias_one=vmem((8, 2, KEYS, 216), f32),
        bias_two=vmem((4, KEYS, 432), f32),
        weight_k=vmem((D1, 256), b16),
        turned_v_one=vmem((D1, D1), b16),
        turned_v_two=vmem((D2, D2), b16),
        weight_q=vmem((D1, 256), b16),
        key_mask=vmem((2, 4, COLUMN, 128), f32),
        query_mask=vmem((2, 2, COLUMN, 128), f32),
        key_mask_two=vmem((2, 2, COLUMN, 128), f32),
        query_mask_two=vmem((2, 2, COLUMN, 128), f32),
        normed_one=vmem((4, COLUMN, D1), f32),
        queries=vmem((2, COLUMN, 256), f32),
        heads=vmem((288, D1), f32),
        ext_two=vmem((2, 2, 144, D2), f32),
        coarse=vmem((2, 72, D2), f32),
        normed_two=vmem((2, 144, D2), f32),
        queries_two=vmem((2, 96, 512), f32),
        heads_two_out=vmem((2, 72, D2), f32),
    )
    held = [vmem(x.shape, x.dtype) for x in fetched.values()]
    sems = dict(
        send=pltpu.SemaphoreType.DMA((35,)),
        recv=pltpu.SemaphoreType.DMA((35,)),
        load=pltpu.SemaphoreType.DMA((len(fetched),)),
    )
    spec = lambda name: pl.BlockSpec(memory_space=pl.ANY if name in fetched else vmem)
    scratch |= sems
    out = pl.pallas_call(
        functools.partial(kernel, lat_size, lon_size, names, tuple(fetched), tuple(scratch)),
        out_shape=jax.ShapeDtypeStruct((6, 6, 4, D2), b16),
        in_specs=[spec(name) for name in names],
        out_specs=pl.BlockSpec(memory_space=vmem),
        scratch_shapes=held + list(scratch.values()),
        compiler_params=pltpu.CompilerParams(
            collective_id=0, has_side_effects=True, vmem_limit_bytes=60 * 1024 * 1024
        ),
        name="block",
    )(*operands.values())
    return out.transpose(2, 0, 1, 3)


def solution(mesh):
    split = P(None, "lat", "lon")
    table = P("lat", None, None, None)
    placed = (P(None, "lat", "lon", None), split, split) + (P(),) * 4 + (table,) + (P(),) * 8 + (table,)
    return jax.shard_map(
        functools.partial(shards, mesh.shape["lat"], mesh.shape["lon"]),
        mesh=mesh,
        in_specs=placed,
        out_specs=P(None, "lat", "lon", None),
        check_vma=False,
    )
```
